128 devices in a mesh: gx: 16 (over y_lo, z, core), gy: 8 (over y_hi, x).
Axes of the slice: x: 4, y: 4 (y_hi: 2, y_lo: 2; y = y_hi * 2 + y_lo), z: 4, core: 2. Of those that a mesh axis runs over, the one named last changes fastest.
Arguments:
- source_now: float32 [128, 128, 1024], P('gx', 'gy'), may hold values from -6 to 6
- source_prev: float32 [128, 128, 1024], P('gx', 'gy'), may hold values from -6 to 6
- receiver_now: float32 [128, 128, 1024], P('gx', 'gy'), may hold values from -6 to 6
- receiver_prev: float32 [128, 128, 1024], P('gx', 'gy'), may hold values from -6 to 6
- velocity_sq: float32 [128, 128, 1024], P('gx', 'gy'), may hold values from 0.02 to 0.18
- source_cells: int32 [4], replicated, may hold values from 0 to 16777215
- source_wavelet: float32 [2, 4], replicated, may hold values from -16 to 16
- receiver_cells: int32 [4096], replicated, may hold values from 0 to 16777215
- receiver_traces: float32 [2, 4096], replicated, may hold values from -12 to 12
Outputs:
- source_next: float32 [128, 128, 1024], P('gx', 'gy')
- receiver_next: float32 [128, 128, 1024], P('gx', 'gy')
- image: float32 [17, 64, 64, 512], P(None, 'gx', 'gy')
The draws below stay inside these ranges and needn't reach their ends.
Inputs may be any that keep to these rules, and one draw needn't show every extreme that they name: `source_cells`: each entry is a flat cell index (x 128 + y) * 1024 + z of the grid; indices may repeat. `receiver_cells`: each entry is a flat cell index (x 128 + y) * 1024 + z of the grid; indices may repeat.
All inputs are finite; a program needn't handle non-finite values.
Results may differ from the reference program's by a relative error of at most 0.00002.
Values sent between devices are 32-bit elements; how exact they have to be, the bound alone decides.
No kernel may reach another device: no remote copies, remote signals or barrier semaphores. Data moves between devices by JAX's collectives and lax.ppermute only.
A program may use at most 128 MiB of HBM per device.

```python
import jax
import jax.numpy as jnp

NZ = 1024
NOFF = 17
STEPS = 2
NSRC = 4
NREC = 4096
NX = 128
NY = 128


def place_ends(result, own_key, smallest, largest):
    extent = result.shape
    place = [jax.random.randint(jax.random.fold_in(own_key, axis), (), 0, extent[axis]) for axis in range(len(extent))]
    result = result.at[tuple(place)].set(smallest)
    longest = extent.index(max(extent))
    place[longest] = (place[longest] + 1) % extent[longest]
    return result.at[tuple(place)].set(largest)


def steps_of(own_key, extent, pieces, low, high):
    factor_of, own = 1.0, jax.random.fold_in(own_key, 6)
    for axis_at, shards_of in pieces:
        draws = jnp.exp(jax.random.uniform(jax.random.fold_in(own, axis_at), (shards_of,), jnp.float32, low / len(pieces), high / len(pieces)))
        factor_of = factor_of * jnp.repeat(draws, extent[axis_at] // shards_of).reshape([-1 if axis == axis_at else 1 for axis in range(len(extent))])
    return factor_of


def normal_values(rng, shape, deviation, limit, pieces=(), held_as=jnp.bfloat16):
    array = deviation * jax.random.normal(rng, shape, jnp.float32)
    if pieces:
        array = array * steps_of(rng, shape, pieces, -0.22, 0.18)
    return jnp.clip(array, -limit, limit).astype(held_as)


def setup_inputs(seed: int = 0) -> dict:
    streams_of = jax.random.split(jax.random.key(seed), 10)
    source_now = normal_values(streams_of[0], (NX, NY, NZ), 1.0, 6.0, ((0, 16), (1, 8)), jnp.float32)
    source_prev = normal_values(streams_of[1], (NX, NY, NZ), 1.0, 6.0, ((0, 16), (1, 8)), jnp.float32)
    receiver_now = normal_values(streams_of[2], (NX, NY, NZ), 1.0, 6.0, ((0, 16), (1, 8)), jnp.float32)
    receiver_prev = normal_values(streams_of[3], (NX, NY, NZ), 1.0, 6.0, ((0, 16), (1, 8)), jnp.float32)
    velocity_sq = jnp.clip(0.02 + 0.16000001 * jax.random.uniform(streams_of[4], (NX, NY, NZ), jnp.float32) ** steps_of(streams_of[4], (NX, NY, NZ), ((0, 16), (1, 8)), -0.2, 0.2), 0.02, 0.18)
    source_cells = place_ends(jax.random.randint(streams_of[5], (NSRC,), 0, NX * NY * NZ), jax.random.fold_in(streams_of[5], 1), 0, (NX * NY * NZ) - 1).astype(jnp.int32)
    source_wavelet = normal_values(streams_of[6], (STEPS, NSRC), 4.0, 16.0, (), jnp.float32)
    receiver_cells = place_ends(jax.random.randint(streams_of[7], (NREC,), 0, NX * NY * NZ), jax.random.fold_in(streams_of[7], 1), 0, (NX * NY * NZ) - 1).astype(jnp.int32)
    receiver_traces = normal_values(streams_of[8], (STEPS, NREC), 2.0, 12.0, (), jnp.float32)
    return dict(source_now=source_now, source_prev=source_prev, receiver_now=receiver_now, receiver_prev=receiver_prev, velocity_sq=velocity_sq, source_cells=source_cells, source_wavelet=source_wavelet, receiver_cells=receiver_cells, receiver_traces=receiver_traces)


COEF = (-205.0 / 72.0, 8.0 / 5.0, -1.0 / 5.0, 8.0 / 315.0, -1.0 / 560.0)


def laplace(field):
    size_x, size_y, size_z = field.shape
    padded = jnp.pad(field, 4)
    total = 3.0 * COEF[0] * field
    for distance in range(1, 5):
        near = padded[4 + distance:4 + distance + size_x, 4:4 + size_y, 4:4 + size_z]
        near = near + padded[4 - distance:4 - distance + size_x, 4:4 + size_y, 4:4 + size_z]
        near = near + padded[4:4 + size_x, 4 + distance:4 + distance + size_y, 4:4 + size_z]
        near = near + padded[4:4 + size_x, 4 - distance:4 - distance + size_y, 4:4 + size_z]
        near = near + padded[4:4 + size_x, 4:4 + size_y, 4 + distance:4 + distance + size_z]
        near = near + padded[4:4 + size_x, 4:4 + size_y, 4 - distance:4 - distance + size_z]
        total = total + COEF[distance] * near
    return total


def inject(cells, amounts):
    flat = jnp.zeros((NX * NY * NZ,), jnp.float32).at[cells].add(amounts.astype(jnp.float32))
    return flat.reshape(NX, NY, NZ)


def offset_image(source_field, receiver_field):
    reach = (NOFF - 1) // 2
    coarse_source = jnp.pad(source_field[:, ::2, ::2], ((reach, reach), (0, 0), (0, 0)))
    coarse_receiver = jnp.pad(receiver_field[:, ::2, ::2], ((reach, reach), (0, 0), (0, 0)))
    gathers = []
    for offset in range(-reach, reach + 1):
        left = coarse_source[reach - offset:reach - offset + NX:2]
        right = coarse_receiver[reach + offset:reach + offset + NX:2]
        gathers.append(left * right)
    return jnp.stack(gathers)


def reference(source_now, source_prev, receiver_now, receiver_prev, velocity_sq, source_cells, source_wavelet, receiver_cells, receiver_traces):
    source_field, source_old = source_now, source_prev
    receiver_field, receiver_old = receiver_now, receiver_prev
    image = jnp.zeros((NOFF, NX // 2, NY // 2, NZ // 2), jnp.float32)
    for instant in range(STEPS):
        source_new = 2.0 * source_field - source_old + velocity_sq * (laplace(source_field) + inject(source_cells, source_wavelet[instant]))
        receiver_new = 2.0 * receiver_field - receiver_old + velocity_sq * (laplace(receiver_field) + inject(receiver_cells, receiver_traces[instant]))
        source_old, source_field = source_field, source_new
        receiver_old, receiver_field = receiver_field, receiver_new
        image = image + offset_image(source_field, receiver_field)
    return source_field, receiver_field, image
```

```python
import jax
import jax.numpy as jnp
from jax import lax
from jax.experimental import pallas as pl
from jax.experimental.pallas import tpu as pltpu
from jax.sharding import PartitionSpec as P

COEF = (-205.0 / 72.0, 8.0 / 5.0, -1.0 / 5.0, 8.0 / 315.0, -1.0 / 560.0)
NOFF = 17
REACH = 8
VX, VY, VZ = 8, 16, 1024
LT = VZ // 128
KT = LT // 2
F32 = jnp.float32

FIELD = (2, VX, LT, VY, 128)
XSLAB = (2, 4, LT, VY, 128)
XSLAB_COARSE = (2, 5, LT, VY, 128)
YSLAB = (2, 4, LT, 8, 128)
COARSE = (2, VX, KT, 8, 128)


def lane_iota(shape):
    return lax.broadcasted_iota(jnp.int32, shape, len(shape) - 1)


def pick(flag, yes, no):
    return jnp.where(flag, yes, no)


def compact_even(first, second):
    lane = lane_iota((8, 128))
    index = (2 * lane) & 127
    left = jnp.take_along_axis(first, index, axis=1)
    right = jnp.take_along_axis(second, index, axis=1)
    return jnp.where(lane < 64, left, right)


def coarse_tile(ref, lead, k):
    first = ref[lead + (2 * k, pl.ds(0, 8, stride=2), slice(None))]
    second = ref[lead + (2 * k + 1, pl.ds(0, 8, stride=2), slice(None))]
    return compact_even(first, second)


def pack_rows(top_ref, bottom_ref, f, l, low, high, gy_even):
    for p in range(VX):
        i, r = p % 4, 4 * (p // 4)
        top_ref[f, i, l, r : r + 4, :] = pick(gy_even, high[p], low[p])
        bottom_ref[f, i, l, r : r + 4, :] = pick(gy_even, low[p], high[p])


def first_pack_kernel(source_ref, receiver_ref, m1, m2, m3, m4):
    gx_even = lax.rem(lax.axis_index("gx"), 2) == 0
    gy_even = lax.rem(lax.axis_index("gy"), 2) == 0

    def tile(l, carry):
        lanes = pl.ds(pl.multiple_of(l * 128, 128), 128)
        for f, ref in enumerate((source_ref, receiver_ref)):
            for p in range(4):
                low = ref[p, :, lanes]
                high = ref[p + 4, :, lanes]
                m1[f, p, l] = pick(gx_even, high, low)
                m2[f, p, l] = pick(gx_even, low, high)
            low = [ref[p, 0:4, lanes] for p in range(VX)]
            high = [ref[p, 12:16, lanes] for p in range(VX)]
            pack_rows(m3, m4, f, l, low, high, gy_even)
        return carry

    lax.fori_loop(0, LT, tile, 0)


def star(ext, f, l, lane):
    centers = [ext[f, p, l + 1, 8 : 8 + VY, :] for p in range(VX)]
    out = []
    for p in range(VX):
        center = centers[p]
        after = ext[f, p, l + 2, 8 : 8 + VY, :]
        before = ext[f, p, l, 8 : 8 + VY, :]
        total = (3.0 * COEF[0]) * center
        for d in range(1, 5):
            near = pltpu.roll(jnp.where(lane >= d, center, after), 128 - d, 1)
            near = near + pltpu.roll(jnp.where(lane < 128 - d, center, before), d, 1)
            near = near + ext[f, p, l + 1, 8 + d : 8 + d + VY, :]
            near = near + ext[f, p, l + 1, 8 - d : 8 - d + VY, :]
            if p + d < VX:
                near = near + centers[p + d]
            if p - d >= 0:
                near = near + centers[p - d]
            total = total + COEF[d] * near
        out.append(total)
    return centers, out


def clear_ext(ext):
    def tile(i, carry):
        f, p = i // VX, lax.rem(i, VX)
        ext[f, p, :, 0:8, :] = jnp.zeros((LT + 2, 8, 128), F32)
        ext[f, p, :, 24:32, :] = jnp.zeros((LT + 2, 8, 128), F32)
        for l in (0, LT + 1):
            ext[f, p, l, 8:24, :] = jnp.zeros((VY, 128), F32)
        return carry

    lax.fori_loop(0, 2 * VX, tile, 0)


def first_local_kernel(
    source_ref,
    receiver_ref,
    source_prev_ref,
    receiver_prev_ref,
    velocity_ref,
    cells_ref,
    source_cells,
    source_wavelet,
    receiver_cells,
    receiver_traces,
    partial_ref,
    inject_ref,
    ext,
    inject_now,
    words_v,
    words_s,
    sem,
):
    anchor_x = lax.axis_index("gx") * VX
    anchor_y = lax.axis_index("gy") * VY

    cells = cells_ref[...]
    local_x = (cells >> 17) - anchor_x
    local_y = ((cells >> 10) & 127) - anchor_y
    inside = (local_x >= 0) & (local_x < VX) & (local_y >= 0) & (local_y < VY)
    bit = jnp.left_shift(1, lax.broadcasted_iota(jnp.int32, (32, 128), 0))
    words_v[...] = jnp.sum(jnp.where(inside, bit, 0), axis=0, keepdims=True)
    copy = pltpu.make_async_copy(words_v, words_s, sem)
    copy.start()

    clear_ext(ext)
    for f, ref in enumerate((source_ref, receiver_ref)):

        def fill(l, carry, f=f, ref=ref):
            lanes = pl.ds(pl.multiple_of(l * 128, 128), 128)
            for p in range(VX):
                ext[f, p, l + 1, 8 : 8 + VY, :] = ref[p, :, lanes]
                inject_ref[f, p, l] = jnp.zeros((VY, 128), F32)
                inject_now[f, p, l] = jnp.zeros((VY, 128), F32)
            return carry

        lax.fori_loop(0, LT, fill, 0)

    row_lane = lane_iota((1, 128))

    def add_point(f, cell, now, later):
        x = lax.shift_right_logical(cell, 17) - anchor_x
        y = (lax.shift_right_logical(cell, 10) & 127) - anchor_y
        z = cell & 1023
        l = lax.shift_right_logical(z, 7)
        here = row_lane == (z & 127)
        for ref, amount in ((inject_now, now), (inject_ref, later)):
            spot = (f, x, l, pl.ds(y, 1), slice(None))
            ref[spot] = ref[spot] + jnp.where(here, amount, 0.0)

    for j in range(source_cells.shape[0]):
        cell = source_cells[j]
        x = lax.shift_right_logical(cell, 17) - anchor_x
        y = (lax.shift_right_logical(cell, 10) & 127) - anchor_y
        here = (x >= 0) & (x < VX) & (y >= 0) & (y < VY)

        @pl.when(here)
        def _(cell=cell, j=j):
            add_point(0, cell, source_wavelet[0, j], source_wavelet[1, j])

    copy.wait()

    def word(w, carry):
        def one(bits):
            low = bits & (-bits)
            j = (31 - lax.clz(low)) * 128 + w
            add_point(1, receiver_cells[j], receiver_traces[0, j], receiver_traces[1, j])
            return bits & (bits - 1)

        lax.while_loop(lambda bits: bits != 0, one, words_s[0, w])
        return carry

    lax.fori_loop(0, 128, word, 0)

    lane = lane_iota((VY, 128))
    for f, older in enumerate((source_prev_ref, receiver_prev_ref)):

        def tile(l, carry, f=f, older=older):
            lanes = pl.ds(pl.multiple_of(l * 128, 128), 128)
            centers, totals = star(ext, f, l, lane)
            for p in range(VX):
                v = velocity_ref[p, :, lanes]
                partial_ref[f, p, l] = (2.0 * centers[p] - older[p, :, lanes]) + v * (totals[p] + inject_now[f, p, l])
            return carry

        lax.fori_loop(0, LT, tile, 0)


def second_local_kernel(now_ref, source_ref, receiver_ref, velocity_ref, inject_ref, partial_ref, ext):
    clear_ext(ext)
    for f in range(2):

        def fill(l, carry, f=f):
            for p in range(VX):
                ext[f, p, l + 1, 8 : 8 + VY, :] = now_ref[f, p, l]
            return carry

        lax.fori_loop(0, LT, fill, 0)
    lane = lane_iota((VY, 128))
    for f, older in enumerate((source_ref, receiver_ref)):

        def tile(l, carry, f=f, older=older):
            lanes = pl.ds(pl.multiple_of(l * 128, 128), 128)
            centers, totals = star(ext, f, l, lane)
            for p in range(VX):
                v = velocity_ref[p, :, lanes]
                partial_ref[f, p, l] = (2.0 * centers[p] - older[p, :, lanes]) + v * (totals[p] + inject_ref[f, p, l])
            return carry

        lax.fori_loop(0, LT, tile, 0)


def halo_terms(m1, m2, m3, m4, rows_low, rows_high, f, l, flags):
    gx_even, has_left, has_right, gy_even, has_below, has_above = flags
    left, right = [], []
    for p in range(4):
        a, b = m1[f, p, l], m2[f, p, l]
        left.append(jnp.where(has_left, pick(gx_even, b, a), 0.0))
        right.append(jnp.where(has_right, pick(gx_even, a, b), 0.0))
    out = []
    for p in range(VX):
        i, r = p % 4, 4 * (p // 4)
        a, b = m3[f, i, l, r : r + 4, :], m4[f, i, l, r : r + 4, :]
        rows_low[p, 0:4, :] = jnp.where(has_below, pick(gy_even, b, a), 0.0)
        rows_high[p, 8:12, :] = jnp.where(has_above, pick(gy_even, a, b), 0.0)
    for p in range(VX):
        below = COEF[1] * rows_low[p, 3:11, :]
        above = COEF[1] * rows_high[p, 1:9, :]
        for d in range(2, 5):
            below = below + COEF[d] * rows_low[p, 4 - d : 12 - d, :]
            above = above + COEF[d] * rows_high[p, d : d + 8, :]
        total = jnp.concatenate((below, above), axis=0)
        for d in range(1, 5):
            if p - d < 0:
                total = total + COEF[d] * left[4 + p - d]
            if p + d >= VX:
                total = total + COEF[d] * right[p + d - VX]
        out.append(total)
    return out


def flags_of():
    gx, gy = lax.axis_index("gx"), lax.axis_index("gy")
    return (
        lax.rem(gx, 2) == 0,
        gx > 0,
        gx < lax.axis_size("gx") - 1,
        lax.rem(gy, 2) == 0,
        gy > 0,
        gy < lax.axis_size("gy") - 1,
    )


def clear_rows(rows_low, rows_high):
    for p in range(VX):
        rows_low[p] = jnp.zeros((16, 128), F32)
        rows_high[p] = jnp.zeros((16, 128), F32)


def first_halo_kernel(
    partial_ref, velocity_ref, m1, m2, m3, m4, now_ref, s1, s2, s3, s4, coarse_ref, rows_low, rows_high
):
    flags = flags_of()
    gx_even, gy_even = flags[0], flags[3]
    clear_rows(rows_low, rows_high)
    for f in range(2):

        def tile(l, carry, f=f):
            lanes = pl.ds(pl.multiple_of(l * 128, 128), 128)
            terms = halo_terms(m1, m2, m3, m4, rows_low, rows_high, f, l, flags)
            new = []
            for p in range(VX):
                value = partial_ref[f, p, l] + velocity_ref[p, :, lanes] * terms[p]
                now_ref[f, p, l] = value
                new.append(value)
            for p in range(4):
                s1[f, p, l] = pick(gx_even, new[p + 4], new[p])
                s2[f, p, l] = pick(gx_even, new[p], new[p + 4])
            pack_rows(s3, s4, f, l, [v[0:4] for v in new], [v[12:16] for v in new], gy_even)
            return carry

        lax.fori_loop(0, LT, tile, 0)
        for k in range(KT):
            low = [coarse_tile(now_ref, (f, p), k) for p in range(4)]
            high = [coarse_tile(now_ref, (f, p + 4), k) for p in range(4)]
            for p in range(4):
                coarse_ref[f, p, k] = low[p]
                coarse_ref[f, p + 4, k] = high[p]
                at = p * KT + k
                rows = slice(8 * (at % 2), 8 * (at % 2) + 8)
                s1[f, 4, at // 2, rows, :] = pick(gx_even, low[p], high[p])
                s2[f, 4, at // 2, rows, :] = pick(gx_even, high[p], low[p])


def second_halo_kernel(
    partial_ref, velocity_ref, m1, m2, m3, m4, source_ref, receiver_ref, coarse_ref, rows_low, rows_high, stage
):
    flags = flags_of()
    clear_rows(rows_low, rows_high)
    for f, out in enumerate((source_ref, receiver_ref)):

        def tile(l, carry, f=f, out=out):
            lanes = pl.ds(pl.multiple_of(l * 128, 128), 128)
            terms = halo_terms(m1, m2, m3, m4, rows_low, rows_high, f, l, flags)
            for p in range(VX):
                value = partial_ref[f, p, l] + velocity_ref[p, :, lanes] * terms[p]
                out[p, :, lanes] = value
                stage[p, l] = value
            return carry

        lax.fori_loop(0, LT, tile, 0)
        for k in range(KT):
            for p in range(VX):
                coarse_ref[f, p, k] = coarse_tile(stage, (p,), k)


def lag_sum(fields, k, write):
    for offset in range(NOFF):
        h = offset - REACH
        for a in range(VX // 2):
            left, right = 2 * a - h + REACH, 2 * a + h + REACH
            write(offset, a, k, sum(s[left] * r[right] for s, r in fields))


def first_image_kernel(coarse_ref, m1, m2, image_ref):
    gx_even, has_left, has_right = flags_of()[:3]

    def planes(f, k):
        left, right = [], []
        near1 = [coarse_tile(m1, (f, p), k) for p in range(4)]
        near2 = [coarse_tile(m2, (f, p), k) for p in range(4)]
        far1, far2 = [], []
        for p in range(4):
            at = p * KT + k
            rows = slice(8 * (at % 2), 8 * (at % 2) + 8)
            far1.append(m1[f, 4, at // 2, rows, :])
            far2.append(m2[f, 4, at // 2, rows, :])
        for far, near in ((0, 1), (1, 0)):
            pass
        for p in range(4):
            left.append(jnp.where(has_left, pick(gx_even, far2[p], far1[p]), 0.0))
        for p in range(4):
            left.append(jnp.where(has_left, pick(gx_even, near2[p], near1[p]), 0.0))
        for p in range(4):
            right.append(jnp.where(has_right, pick(gx_even, near1[p], near2[p]), 0.0))
        for p in range(4):
            right.append(jnp.where(has_right, pick(gx_even, far1[p], far2[p]), 0.0))
        return left + [coarse_ref[f, p, k] for p in range(VX)] + right

    for k in range(KT):

        def write(o, a, k, value):
            image_ref[o, a, k] = value

        lag_sum([(planes(0, k), planes(1, k))], k, write)


def second_image_kernel(coarse_ref, m1, m2, before_ref, image_ref):
    gx_even, has_left, has_right = flags_of()[:3]

    def planes(f, k):
        left, right = [], []
        for p in range(VX):
            a, b = m1[f, p, k], m2[f, p, k]
            left.append(jnp.where(has_left, pick(gx_even, b, a), 0.0))
            right.append(jnp.where(has_right, pick(gx_even, a, b), 0.0))
        return left + [coarse_ref[f, p, k] for p in range(VX)] + right

    for k in range(KT):

        def write(o, a, k, value):
            image_ref[o, a, :, k * 128 : (k + 1) * 128] = before_ref[o, a, k] + value

        lag_sum([(planes(0, k), planes(1, k))], k, write)


VMEM = pl.BlockSpec(memory_space=pltpu.VMEM)
SMEM = pl.BlockSpec(memory_space=pltpu.SMEM)


def call(kernel, ins, outs, scratch=(), name=None, cost=0, limit=12):
    return pl.pallas_call(
        kernel,
        out_shape=[jax.ShapeDtypeStruct(s, F32) for s in outs],
        in_specs=[s for s, _ in ins],
        out_specs=[VMEM] * len(outs),
        scratch_shapes=list(scratch),
        name=name,
        cost_estimate=pl.CostEstimate(flops=cost, bytes_accessed=4 << 20, transcendentals=0),
        compiler_params=pltpu.CompilerParams(vmem_limit_bytes=limit << 20),
    )(*[a for _, a in ins])


def vmem(*arrays):
    return [(VMEM, a) for a in arrays]


def smem(*arrays):
    return [(SMEM, a) for a in arrays]


def matchings(axis):
    n = lax.axis_size(axis)
    inner = [(i, i ^ 1) for i in range(n)]
    outer = [(i, (i + 1) % n if i % 2 else (i - 1) % n) for i in range(n)]
    return inner, outer


def exchange(m1, m2, m3=None, m4=None):
    x_in, x_out = matchings("gx")
    y_in, y_out = matchings("gy")
    g2 = lax.ppermute(m2, "gx", x_out)
    if m3 is not None:
        g4 = lax.ppermute(m4, "gy", y_out)
        g3 = lax.ppermute(m3, "gy", y_in)
    g1 = lax.ppermute(m1, "gx", x_in)
    if m3 is None:
        return g1, g2
    return g1, g2, g3, g4


def local(
    source_now,
    source_prev,
    receiver_now,
    receiver_prev,
    velocity_sq,
    source_cells,
    source_wavelet,
    receiver_cells,
    receiver_traces,
):
    ext = pltpu.VMEM((2, VX, LT + 2, 32, 128), F32)
    rows = pltpu.VMEM((VX, 16, 128), F32)
    sends = call(
        first_pack_kernel, vmem(source_now, receiver_now), (XSLAB, XSLAB, YSLAB, YSLAB), name="pack"
    )
    got = exchange(*sends)
    partial, inject = call(
        first_local_kernel,
        vmem(source_now, receiver_now, source_prev, receiver_prev, velocity_sq, receiver_cells.reshape(32, 128))
        + smem(source_cells, source_wavelet, receiver_cells, receiver_traces),
        (FIELD, FIELD),
        (
            ext,
            pltpu.VMEM(FIELD, F32),
            pltpu.VMEM((1, 128), jnp.int32),
            pltpu.SMEM((1, 128), jnp.int32),
            pltpu.SemaphoreType.DMA,
        ),
        name="local1",
        cost=20_000_000,
    )
    now, s1, s2, s3, s4, coarse = call(
        first_halo_kernel,
        vmem(partial, velocity_sq, *got),
        (FIELD, XSLAB_COARSE, XSLAB_COARSE, YSLAB, YSLAB, COARSE),
        (rows, rows),
        name="halo1",
    )
    got = exchange(s1, s2, s3, s4)
    (partial,) = call(
        second_local_kernel,
        vmem(now, source_now, receiver_now, velocity_sq, inject),
        (FIELD,),
        (ext,),
        name="local2",
        cost=20_000_000,
    )
    source_next, receiver_next, last = call(
        second_halo_kernel,
        vmem(partial, velocity_sq, *got),
        ((VX, VY, VZ), (VX, VY, VZ), COARSE),
        (rows, rows, pltpu.VMEM((VX, LT, VY, 128), F32)),
        name="halo2",
    )
    far = exchange(last, last)
    (image,) = call(
        first_image_kernel, vmem(coarse, got[0], got[1]), ((NOFF, VX // 2, KT, 8, 128),), name="image1", cost=5_000_000
    )
    (image,) = call(
        second_image_kernel, vmem(last, *far, image), ((NOFF, VX // 2, 8, KT * 128),), name="image2"
    )
    return source_next, receiver_next, image


def solution(mesh):
    field = P("gx", "gy", None)
    return jax.shard_map(
        local,
        mesh=mesh,
        in_specs=(field,) * 5 + (P(),) * 4,
        out_specs=(field, field, P(None, "gx", "gy", None)),
        check_vma=False,
    )
```

```python
import jax
import jax.numpy as jnp
from jax import lax
from jax.experimental import pallas as pl
from jax.experimental.pallas import tpu as pltpu
from jax.sharding import PartitionSpec as P

COEF = (-205.0 / 72.0, 8.0 / 5.0, -1.0 / 5.0, 8.0 / 315.0, -1.0 / 560.0)
NOFF = 17
REACH = 8
VX, VY, VZ = 8, 16, 1024
LT = VZ // 128
KT = LT // 2
F32 = jnp.float32

FIELD = (2, VX, LT, VY, 128)
XSLAB = (2, 4, LT, VY, 128)
XSLAB_COARSE = (2, 5, LT, VY, 128)
YSLAB = (2, 4, LT, 8, 128)
COARSE = (2, VX, KT, 8, 128)


def lane_iota(shape):
    return lax.broadcasted_iota(jnp.int32, shape, len(shape) - 1)


def pick(flag, yes, no):
    return jnp.where(flag, yes, no)


def compact_even(first, second):
    lane = lane_iota((8, 128))
    index = (2 * lane) & 127
    left = jnp.take_along_axis(first, index, axis=1)
    right = jnp.take_along_axis(second, index, axis=1)
    return jnp.where(lane < 64, left, right)


def coarse_tile(ref, lead, k):
    first = ref[lead + (2 * k, pl.ds(0, 8, stride=2), slice(None))]
    second = ref[lead + (2 * k + 1, pl.ds(0, 8, stride=2), slice(None))]
    return compact_even(first, second)


def pack_rows(top_ref, bottom_ref, f, l, low, high, gy_even):
    for p in range(VX):
        i, r = p % 4, 4 * (p // 4)
        top_ref[f, i, l, r : r + 4, :] = pick(gy_even, high[p], low[p])
        bottom_ref[f, i, l, r : r + 4, :] = pick(gy_even, low[p], high[p])


def first_pack_kernel(source_hbm, receiver_hbm, m1, m2, m3, m4, source_ref, receiver_ref, sems):
    gx_even = lax.rem(lax.axis_index("gx"), 2) == 0
    gy_even = lax.rem(lax.axis_index("gy"), 2) == 0
    copies = [
        pltpu.make_async_copy(source_hbm, source_ref, sems.at[0]),
        pltpu.make_async_copy(receiver_hbm, receiver_ref, sems.at[1]),
    ]
    for copy in copies:
        copy.start()

    for f, ref in enumerate((source_ref, receiver_ref)):
        copies[f].wait()

        def tile(l, carry, f=f, ref=ref):
            lanes = pl.ds(pl.multiple_of(l * 128, 128), 128)
            for p in range(4):
                low = ref[p, :, lanes]
                high = ref[p + 4, :, lanes]
                m1[f, p, l] = pick(gx_even, high, low)
                m2[f, p, l] = pick(gx_even, low, high)
            low = [ref[p, 0:4, lanes] for p in range(VX)]
            high = [ref[p, 12:16, lanes] for p in range(VX)]
            pack_rows(m3, m4, f, l, low, high, gy_even)
            return carry

        lax.fori_loop(0, LT, tile, 0)


def star(ext, f, l, lane):
    centers = [ext[f, p, l + 1, 8 : 8 + VY, :] for p in range(VX)]
    out = []
    for p in range(VX):
        center = centers[p]
        after = ext[f, p, l + 2, 8 : 8 + VY, :]
        before = ext[f, p, l, 8 : 8 + VY, :]
        total = (3.0 * COEF[0]) * center
        for d in range(1, 5):
            near = pltpu.roll(jnp.where(lane >= d, center, after), 128 - d, 1)
            near = near + pltpu.roll(jnp.where(lane < 128 - d, center, before), d, 1)
            near = near + ext[f, p, l + 1, 8 + d : 8 + d + VY, :]
            near = near + ext[f, p, l + 1, 8 - d : 8 - d + VY, :]
            if p + d < VX:
                near = near + centers[p + d]
            if p - d >= 0:
                near = near + centers[p - d]
            total = total + COEF[d] * near
        out.append(total)
    return centers, out


def clear_ext(ext):
    def tile(i, carry):
        f, p = i // VX, lax.rem(i, VX)
        ext[f, p, :, 0:8, :] = jnp.zeros((LT + 2, 8, 128), F32)
        ext[f, p, :, 24:32, :] = jnp.zeros((LT + 2, 8, 128), F32)
        for l in (0, LT + 1):
            ext[f, p, l, 8:24, :] = jnp.zeros((VY, 128), F32)
        return carry

    lax.fori_loop(0, 2 * VX, tile, 0)


def first_local_kernel(
    source_ref,
    receiver_ref,
    source_prev_hbm,
    receiver_prev_hbm,
    velocity_hbm,
    cells_hbm,
    source_cells_hbm,
    source_wavelet_hbm,
    receiver_cells_hbm,
    receiver_traces_hbm,
    partial_ref,
    inject_ref,
    velocity_ref,
    ext,
    inject_now,
    source_prev_ref,
    receiver_prev_ref,
    cells_ref,
    source_cells,
    source_wavelet,
    receiver_cells,
    receiver_traces,
    words_v,
    words_s,
    sems,
    word_sem,
):
    anchor_x = lax.axis_index("gx") * VX
    anchor_y = lax.axis_index("gy") * VY

    pairs = (
        (cells_hbm, cells_ref),
        (source_cells_hbm, source_cells),
        (source_wavelet_hbm, source_wavelet),
        (receiver_cells_hbm, receiver_cells),
        (receiver_traces_hbm, receiver_traces),
        (velocity_hbm, velocity_ref),
        (source_prev_hbm, source_prev_ref),
        (receiver_prev_hbm, receiver_prev_ref),
    )
    copies = [pltpu.make_async_copy(a, b, sems.at[i]) for i, (a, b) in enumerate(pairs)]
    for copy in copies:
        copy.start()

    clear_ext(ext)
    for f, ref in enumerate((source_ref, receiver_ref)):

        def fill(l, carry, f=f, ref=ref):
            lanes = pl.ds(pl.multiple_of(l * 128, 128), 128)
            for p in range(VX):
                ext[f, p, l + 1, 8 : 8 + VY, :] = ref[p, :, lanes]
                inject_ref[f, p, l] = jnp.zeros((VY, 128), F32)
                inject_now[f, p, l] = jnp.zeros((VY, 128), F32)
            return carry

        lax.fori_loop(0, LT, fill, 0)

    copies[0].wait()
    cells = cells_ref[...]
    local_x = (cells >> 17) - anchor_x
    local_y = ((cells >> 10) & 127) - anchor_y
    inside = (local_x >= 0) & (local_x < VX) & (local_y >= 0) & (local_y < VY)
    bit = jnp.left_shift(1, lax.broadcasted_iota(jnp.int32, (32, 128), 0))
    words_v[...] = jnp.sum(jnp.where(inside, bit, 0), axis=0, keepdims=True)
    word_copy = pltpu.make_async_copy(words_v, words_s, word_sem)
    word_copy.start()
    for copy in copies[1:]:
        copy.wait()

    row_lane = lane_iota((1, 128))

    def add_point(f, cell, now, later):
        x = lax.shift_right_logical(cell, 17) - anchor_x
        y = (lax.shift_right_logical(cell, 10) & 127) - anchor_y
        z = cell & 1023
        l = lax.shift_right_logical(z, 7)
        here = row_lane == (z & 127)
        for ref, amount in ((inject_now, now), (inject_ref, later)):
            spot = (f, x, l, pl.ds(y, 1), slice(None))
            ref[spot] = ref[spot] + jnp.where(here, amount, 0.0)

    for j in range(source_cells.shape[0]):
        cell = source_cells[j]
        x = lax.shift_right_logical(cell, 17) - anchor_x
        y = (lax.shift_right_logical(cell, 10) & 127) - anchor_y
        here = (x >= 0) & (x < VX) & (y >= 0) & (y < VY)

        @pl.when(here)
        def _(cell=cell, j=j):
            add_point(0, cell, source_wavelet[0, j], source_wavelet[1, j])

    word_copy.wait()

    def word(w, carry):
        def one(bits):
            low = bits & (-bits)
            j = (31 - lax.clz(low)) * 128 + w
            add_point(1, receiver_cells[j], receiver_traces[0, j], receiver_traces[1, j])
            return bits & (bits - 1)

        lax.while_loop(lambda bits: bits != 0, one, words_s[0, w])
        return carry

    lax.fori_loop(0, 128, word, 0)

    lane = lane_iota((VY, 128))
    for f, older in enumerate((source_prev_ref, receiver_prev_ref)):

        def tile(l, carry, f=f, older=older):
            lanes = pl.ds(pl.multiple_of(l * 128, 128), 128)
            centers, totals = star(ext, f, l, lane)
            for p in range(VX):
                v = velocity_ref[p, :, lanes]
                partial_ref[f, p, l] = (2.0 * centers[p] - older[p, :, lanes]) + v * (totals[p] + inject_now[f, p, l])
            return carry

        lax.fori_loop(0, LT, tile, 0)


def second_local_kernel(now_ref, source_ref, receiver_ref, velocity_ref, inject_ref, partial_ref, ext):
    clear_ext(ext)
    for f in range(2):

        def fill(l, carry, f=f):
            for p in range(VX):
                ext[f, p, l + 1, 8 : 8 + VY, :] = now_ref[f, p, l]
            return carry

        lax.fori_loop(0, LT, fill, 0)
    lane = lane_iota((VY, 128))
    for f, older in enumerate((source_ref, receiver_ref)):

        def tile(l, carry, f=f, older=older):
            lanes = pl.ds(pl.multiple_of(l * 128, 128), 128)
            centers, totals = star(ext, f, l, lane)
            for p in range(VX):
                v = velocity_ref[p, :, lanes]
                partial_ref[f, p, l] = (2.0 * centers[p] - older[p, :, lanes]) + v * (totals[p] + inject_ref[f, p, l])
            return carry

        lax.fori_loop(0, LT, tile, 0)


def halo_terms(m1, m2, m3, m4, rows_low, rows_high, f, l, flags):
    gx_even, has_left, has_right, gy_even, has_below, has_above = flags
    left, right = [], []
    for p in range(4):
        a, b = m1[f, p, l], m2[f, p, l]
        left.append(jnp.where(has_left, pick(gx_even, b, a), 0.0))
        right.append(jnp.where(has_right, pick(gx_even, a, b), 0.0))
    out = []
    for p in range(VX):
        i, r = p % 4, 4 * (p // 4)
        a, b = m3[f, i, l, r : r + 4, :], m4[f, i, l, r : r + 4, :]
        rows_low[p, 0:4, :] = jnp.where(has_below, pick(gy_even, b, a), 0.0)
        rows_high[p, 8:12, :] = jnp.where(has_above, pick(gy_even, a, b), 0.0)
    for p in range(VX):
        below = COEF[1] * rows_low[p, 3:11, :]
        above = COEF[1] * rows_high[p, 1:9, :]
        for d in range(2, 5):
            below = below + COEF[d] * rows_low[p, 4 - d : 12 - d, :]
            above = above + COEF[d] * rows_high[p, d : d + 8, :]
        total = jnp.concatenate((below, above), axis=0)
        for d in range(1, 5):
            if p - d < 0:
                total = total + COEF[d] * left[4 + p - d]
            if p + d >= VX:
                total = total + COEF[d] * right[p + d - VX]
        out.append(total)
    return out


def flags_of():
    gx, gy = lax.axis_index("gx"), lax.axis_index("gy")
    return (
        lax.rem(gx, 2) == 0,
        gx > 0,
        gx < lax.axis_size("gx") - 1,
        lax.rem(gy, 2) == 0,
        gy > 0,
        gy < lax.axis_size("gy") - 1,
    )


def clear_rows(rows_low, rows_high):
    for p in range(VX):
        rows_low[p] = jnp.zeros((16, 128), F32)
        rows_high[p] = jnp.zeros((16, 128), F32)


def first_halo_kernel(
    partial_ref, velocity_ref, m1, m2, m3, m4, now_ref, s1, s2, s3, s4, coarse_ref, rows_low, rows_high
):
    flags = flags_of()
    gx_even, gy_even = flags[0], flags[3]
    clear_rows(rows_low, rows_high)
    for f in range(2):

        def tile(l, carry, f=f):
            lanes = pl.ds(pl.multiple_of(l * 128, 128), 128)
            terms = halo_terms(m1, m2, m3, m4, rows_low, rows_high, f, l, flags)
            new = []
            for p in range(VX):
                value = partial_ref[f, p, l] + velocity_ref[p, :, lanes] * terms[p]
                now_ref[f, p, l] = value
                new.append(value)
            for p in range(4):
                s1[f, p, l] = pick(gx_even, new[p + 4], new[p])
                s2[f, p, l] = pick(gx_even, new[p], new[p + 4])
            pack_rows(s3, s4, f, l, [v[0:4] for v in new], [v[12:16] for v in new], gy_even)
            return carry

        lax.fori_loop(0, LT, tile, 0)
        for k in range(KT):
            low = [coarse_tile(now_ref, (f, p), k) for p in range(4)]
            high = [coarse_tile(now_ref, (f, p + 4), k) for p in range(4)]
            for p in range(4):
                coarse_ref[f, p, k] = low[p]
                coarse_ref[f, p + 4, k] = high[p]
                at = p * KT + k
                rows = slice(8 * (at % 2), 8 * (at % 2) + 8)
                s1[f, 4, at // 2, rows, :] = pick(gx_even, low[p], high[p])
                s2[f, 4, at // 2, rows, :] = pick(gx_even, high[p], low[p])


def second_halo_kernel(
    partial_ref, velocity_ref, m1, m2, m3, m4, source_ref, receiver_ref, coarse_ref, rows_low, rows_high, stage
):
    flags = flags_of()
    clear_rows(rows_low, rows_high)
    for f, out in enumerate((source_ref, receiver_ref)):

        def tile(l, carry, f=f, out=out):
            lanes = pl.ds(pl.multiple_of(l * 128, 128), 128)
            terms = halo_terms(m1, m2, m3, m4, rows_low, rows_high, f, l, flags)
            for p in range(VX):
                value = partial_ref[f, p, l] + velocity_ref[p, :, lanes] * terms[p]
                out[p, :, lanes] = value
                stage[p, l] = value
            return carry

        lax.fori_loop(0, LT, tile, 0)
        for k in range(KT):
            for p in range(VX):
                coarse_ref[f, p, k] = coarse_tile(stage, (p,), k)


def first_image_kernel(coarse_ref, m1, m2, source_ref, receiver_ref, image_ref, source_hbm, receiver_hbm, sems):
    gx_even, has_left, has_right = flags_of()[:3]
    copies = [
        pltpu.make_async_copy(source_ref, source_hbm, sems.at[0]),
        pltpu.make_async_copy(receiver_ref, receiver_hbm, sems.at[1]),
    ]
    for copy in copies:
        copy.start()

    def planes(f, k):
        left, right = [], []
        near1 = [coarse_tile(m1, (f, p), k) for p in range(4)]
        near2 = [coarse_tile(m2, (f, p), k) for p in range(4)]
        far1, far2 = [], []
        for p in range(4):
            at = p * KT + k
            rows = slice(8 * (at % 2), 8 * (at % 2) + 8)
            far1.append(m1[f, 4, at // 2, rows, :])
            far2.append(m2[f, 4, at // 2, rows, :])
        for p in range(4):
            left.append(jnp.where(has_left, pick(gx_even, far2[p], far1[p]), 0.0))
        for p in range(4):
            left.append(jnp.where(has_left, pick(gx_even, near2[p], near1[p]), 0.0))
        for p in range(4):
            right.append(jnp.where(has_right, pick(gx_even, near1[p], near2[p]), 0.0))
        for p in range(4):
            right.append(jnp.where(has_right, pick(gx_even, far1[p], far2[p]), 0.0))
        return left + [coarse_ref[f, p, k] for p in range(VX)] + right

    for k in range(KT):
        source, receiver = planes(0, k), planes(1, k)
        for offset in range(NOFF):
            h = offset - REACH
            for a in range(VX // 2):
                image_ref[offset, a, k] = source[2 * a - h + REACH] * receiver[2 * a + h + REACH]
    for copy in copies:
        copy.wait()


def second_image_kernel(coarse_ref, m1, m2, before_ref, image_hbm, span, stage, sems):
    gx_even, has_left, has_right = flags_of()[:3]
    for f in range(2):
        for p in range(VX):
            span[f, p + REACH] = coarse_ref[f, p]
            for k in range(KT):
                a, b = m1[f, p, k], m2[f, p, k]
                span[f, p, k] = jnp.where(has_left, pick(gx_even, b, a), 0.0)
                span[f, p + REACH + VX, k] = jnp.where(has_right, pick(gx_even, a, b), 0.0)

    copies = []
    for a in range(VX // 2):
        for offset in range(NOFF):
            h = offset - REACH
            left, right = 2 * a - h + REACH, 2 * a + h + REACH
            for k in range(KT):
                value = before_ref[offset, a, k] + span[0, left, k] * span[1, right, k]
                stage[offset, a, :, k * 128 : (k + 1) * 128] = value
        copy = pltpu.make_async_copy(stage.at[:, a], image_hbm.at[:, a], sems.at[a])
        copy.start()
        copies.append(copy)
    for copy in copies:
        copy.wait()


VMEM = pl.BlockSpec(memory_space=pltpu.VMEM)
HBM = pl.BlockSpec(memory_space=pltpu.HBM)


def call(kernel, ins, outs, scratch=(), name=None, cost=0, limit=12):
    return pl.pallas_call(
        kernel,
        out_shape=[jax.ShapeDtypeStruct(s, F32) for _, s in outs],
        in_specs=[s for s, _ in ins],
        out_specs=[s for s, _ in outs],
        scratch_shapes=list(scratch),
        name=name,
        cost_estimate=pl.CostEstimate(flops=cost, bytes_accessed=4 << 20, transcendentals=0),
        compiler_params=pltpu.CompilerParams(vmem_limit_bytes=limit << 20),
    )(*[pltpu.with_memory_space_constraint(a, pltpu.HBM) if s is HBM else a for s, a in ins])


def vmem(*items):
    return [(VMEM, a) for a in items]


def hbm(*items):
    return [(HBM, a) for a in items]


def dma(count):
    return pltpu.SemaphoreType.DMA((count,))


def matchings(axis):
    n = lax.axis_size(axis)
    inner = [(i, i ^ 1) for i in range(n)]
    outer = [(i, (i + 1) % n if i % 2 else (i - 1) % n) for i in range(n)]
    return inner, outer


def y_outer():
    nx, ny = lax.axis_size("gx"), lax.axis_size("gy")
    pairs = []
    for x in range(nx):
        for y in range(ny):
            other = y + 1 if y % 2 else y - 1
            if 0 <= other < ny:
                pairs.append((x * ny + y, x * ny + other))
            else:
                pairs.append((x * ny + y, (x ^ 1) * ny + y))
    return pairs


def exchange(m1, m2, m3=None, m4=None):
    x_in, x_out = matchings("gx")
    y_in, _ = matchings("gy")
    g2 = lax.ppermute(m2, "gx", x_out)
    if m3 is not None:
        g4 = lax.ppermute(m4, ("gx", "gy"), y_outer())
        g3 = lax.ppermute(m3, "gy", y_in)
    g1 = lax.ppermute(m1, "gx", x_in)
    if m3 is None:
        return g1, g2
    return g1, g2, g3, g4


def local(
    source_now,
    source_prev,
    receiver_now,
    receiver_prev,
    velocity_sq,
    source_cells,
    source_wavelet,
    receiver_cells,
    receiver_traces,
):
    ext = pltpu.VMEM((2, VX, LT + 2, 32, 128), F32)
    rows = pltpu.VMEM((VX, 16, 128), F32)
    block = (VX, VY, VZ)
    *sends, source, receiver = call(
        first_pack_kernel,
        hbm(source_now, receiver_now),
        vmem(XSLAB, XSLAB, YSLAB, YSLAB, block, block),
        (dma(2),),
        name="pack",
    )
    got = exchange(*sends)
    partial, inject, velocity = call(
        first_local_kernel,
        vmem(source, receiver)
        + hbm(source_prev, receiver_prev, velocity_sq, receiver_cells.reshape(32, 128))
        + hbm(source_cells, source_wavelet, receiver_cells, receiver_traces),
        vmem(FIELD, FIELD, block),
        (
            ext,
            pltpu.VMEM(FIELD, F32),
            pltpu.VMEM(block, F32),
            pltpu.VMEM(block, F32),
            pltpu.VMEM((32, 128), jnp.int32),
            pltpu.SMEM(source_cells.shape, jnp.int32),
            pltpu.SMEM(source_wavelet.shape, F32),
            pltpu.SMEM(receiver_cells.shape, jnp.int32),
            pltpu.SMEM(receiver_traces.shape, F32),
            pltpu.VMEM((1, 128), jnp.int32),
            pltpu.SMEM((1, 128), jnp.int32),
            dma(8),
            pltpu.SemaphoreType.DMA,
        ),
        name="local1",
        cost=20_000_000,
    )
    now, s1, s2, s3, s4, coarse = call(
        first_halo_kernel,
        vmem(partial, velocity, *got),
        vmem(FIELD, XSLAB_COARSE, XSLAB_COARSE, YSLAB, YSLAB, COARSE),
        (rows, rows),
        name="halo1",
    )
    got = exchange(s1, s2, s3, s4)
    (partial,) = call(
        second_local_kernel,
        vmem(now, source, receiver, velocity, inject),
        vmem(FIELD),
        (ext,),
        name="local2",
        cost=20_000_000,
    )
    source, receiver, last = call(
        second_halo_kernel,
        vmem(partial, velocity, *got),
        vmem(block, block, COARSE),
        (rows, rows, pltpu.VMEM((VX, LT, VY, 128), F32)),
        name="halo2",
    )
    far = exchange(last, last)
    image, source_next, receiver_next = call(
        first_image_kernel,
        vmem(coarse, got[0], got[1], source, receiver),
        vmem((NOFF, VX // 2, KT, 8, 128)) + hbm(block, block),
        (dma(2),),
        name="image1",
        cost=5_000_000,
    )
    (image,) = call(
        second_image_kernel,
        vmem(last, *far, image),
        hbm((NOFF, VX // 2, 8, KT * 128)),
        (
            pltpu.VMEM((2, 2 * REACH + VX, KT, 8, 128), F32),
            pltpu.VMEM((NOFF, VX // 2, 8, KT * 128), F32),
            dma(VX // 2),
        ),
        name="image2",
    )
    return source_next, receiver_next, image


def solution(mesh):
    field = P("gx", "gy", None)
    return jax.shard_map(
        local,
        mesh=mesh,
        in_specs=(field,) * 5 + (P(),) * 4,
        out_specs=(field, field, P(None, "gx", "gy", None)),
        check_vma=False,
    )
```

```python
import functools

import jax
import jax.numpy as jnp
from jax import lax
from jax.experimental import pallas as pl
from jax.experimental.pallas import tpu as pltpu
from jax.sharding import PartitionSpec as P

COEF = (-205.0 / 72.0, 8.0 / 5.0, -1.0 / 5.0, 8.0 / 315.0, -1.0 / 560.0)
NOFF = 17
REACH = 8
VX, VY, VZ = 8, 16, 1024
LT = VZ // 128
KT = LT // 2
F32 = jnp.float32

FIELD = (VX, LT, VY, 128)
XSLAB = (2, 4, LT, VY, 128)
XSLAB_COARSE = (2, 5, LT, VY, 128)
YSLAB = (2, 4, LT, 8, 128)
COARSE = (2, VX, KT, 8, 128)


def lane_iota(shape):
    return lax.broadcasted_iota(jnp.int32, shape, len(shape) - 1)


def pick(flag, yes, no):
    return jnp.where(flag, yes, no)


def compact_even(first, second):
    lane = lane_iota((8, 128))
    index = (2 * lane) & 127
    left = jnp.take_along_axis(first, index, axis=1)
    right = jnp.take_along_axis(second, index, axis=1)
    return jnp.where(lane < 64, left, right)


def coarse_tile(ref, lead, k):
    first = ref[lead + (2 * k, pl.ds(0, 8, stride=2), slice(None))]
    second = ref[lead + (2 * k + 1, pl.ds(0, 8, stride=2), slice(None))]
    return compact_even(first, second)


def pack_rows(top_ref, bottom_ref, f, l, low, high, gy_even):
    for p in range(VX):
        i, r = p % 4, 4 * (p // 4)
        top_ref[f, i, l, r : r + 4, :] = pick(gy_even, high[p], low[p])
        bottom_ref[f, i, l, r : r + 4, :] = pick(gy_even, low[p], high[p])


def first_pack_kernel(
    source_hbm,
    receiver_hbm,
    m1,
    m2,
    m3,
    m4,
    source_ref,
    receiver_ref,
    sems,
):
    gx_even = lax.rem(lax.axis_index("gx"), 2) == 0
    gy_even = lax.rem(lax.axis_index("gy"), 2) == 0
    copies = start_all(((source_hbm, source_ref), (receiver_hbm, receiver_ref)), sems)
    for f, ref in enumerate((source_ref, receiver_ref)):
        copies[f].wait()

        def tile(l, carry, f=f, ref=ref):
            lanes = pl.ds(pl.multiple_of(l * 128, 128), 128)
            for p in range(4):
                low = ref[p, :, lanes]
                high = ref[p + 4, :, lanes]
                m1[f, p, l] = pick(gx_even, high, low)
                m2[f, p, l] = pick(gx_even, low, high)
            low = [ref[p, 0:4, lanes] for p in range(VX)]
            high = [ref[p, 12:16, lanes] for p in range(VX)]
            pack_rows(m3, m4, f, l, low, high, gy_even)
            return carry

        lax.fori_loop(0, LT, tile, 0)


def star(ext, l, lane):
    centers = [ext[p, l + 1, 8 : 8 + VY, :] for p in range(VX)]
    out = []
    for p in range(VX):
        center = centers[p]
        after = ext[p, l + 2, 8 : 8 + VY, :]
        before = ext[p, l, 8 : 8 + VY, :]
        total = (3.0 * COEF[0]) * center
        for d in range(1, 5):
            near = pltpu.roll(jnp.where(lane >= d, center, after), 128 - d, 1)
            near = near + pltpu.roll(jnp.where(lane < 128 - d, center, before), d, 1)
            near = near + ext[p, l + 1, 8 + d : 8 + d + VY, :]
            near = near + ext[p, l + 1, 8 - d : 8 - d + VY, :]
            if p + d < VX:
                near = near + centers[p + d]
            if p - d >= 0:
                near = near + centers[p - d]
            total = total + COEF[d] * near
        out.append(total)
    return centers, out


def clear_ext(ext):
    def tile(p, carry):
        ext[p, :, 0:8, :] = jnp.zeros((LT + 2, 8, 128), F32)
        ext[p, :, 24:32, :] = jnp.zeros((LT + 2, 8, 128), F32)
        for l in (0, LT + 1):
            ext[p, l, 8:24, :] = jnp.zeros((VY, 128), F32)
        return carry

    lax.fori_loop(0, VX, tile, 0)


def lanes_of(l):
    return pl.ds(pl.multiple_of(l * 128, 128), 128)


def locate(cell):
    x = lax.shift_right_logical(cell, 17) - lax.axis_index("gx") * VX
    y = (lax.shift_right_logical(cell, 10) & 127) - lax.axis_index("gy") * VY
    return x, y, cell & 1023


def add_point(ref, cell, amount, velocity_ref=None):
    x, y, z = locate(cell)
    l = lax.shift_right_logical(z, 7)
    value = jnp.full((VY, 128), amount, F32)
    if velocity_ref is not None:
        value = value * velocity_ref[x, :, lanes_of(l)]
    row = lax.broadcasted_iota(jnp.int32, (VY, 128), 0)
    here = (row == y) & (lane_iota((VY, 128)) == (z & 127))
    ref[x, l] = ref[x, l] + jnp.where(here, value, 0.0)


def add_sources(ref, cells, wavelet, instant, velocity_ref):
    for j in range(cells.shape[0]):
        cell = cells[j]
        x, y, _ = locate(cell)
        here = (x >= 0) & (x < VX) & (y >= 0) & (y < VY)

        @pl.when(here)
        def _(cell=cell, j=j):
            add_point(ref, cell, wavelet[instant, j], velocity_ref)


def stencil(ext, older, velocity_ref, partial_ref, inject_ref=None):
    lane = lane_iota((VY, 128))

    def tile(l, carry):
        centers, totals = star(ext, l, lane)
        for p in range(VX):
            total = totals[p]
            if inject_ref is not None:
                total = total + inject_ref[p, l]
            v = velocity_ref[p, :, lanes_of(l)]
            partial_ref[p, l] = (2.0 * centers[p] - older[p, :, lanes_of(l)]) + v * total
        return carry

    lax.fori_loop(0, LT, tile, 0)


def start_all(pairs, sems):
    copies = [pltpu.make_async_copy(a, b, sems.at[i]) for i, (a, b) in enumerate(pairs)]
    for copy in copies:
        copy.start()
    return copies


def fill_ext(ext, ref):
    def tile(l, carry):
        for p in range(VX):
            ext[p, l + 1, 8 : 8 + VY, :] = ref[p, :, lanes_of(l)]
        return carry

    lax.fori_loop(0, LT, tile, 0)


def fill_ext_tiled(ext, ref):
    def tile(l, carry):
        for p in range(VX):
            ext[p, l + 1, 8 : 8 + VY, :] = ref[p, l]
        return carry

    lax.fori_loop(0, LT, tile, 0)


def first_receiver_kernel(
    now_ref,
    velocity_ref,
    prev_hbm,
    grid_hbm,
    cells_hbm,
    traces_hbm,
    partial_ref,
    inject_ref,
    ext,
    prev_ref,
    grid_ref,
    cells,
    traces,
    words_v,
    words_s,
    sems,
    word_sem,
):
    copies = start_all(
        ((grid_hbm, grid_ref), (cells_hbm, cells), (traces_hbm, traces), (prev_hbm, prev_ref)), sems
    )
    clear_ext(ext)
    fill_ext(ext, now_ref)

    copies[0].wait()
    x, y, _ = locate(grid_ref[...])
    inside = (x >= 0) & (x < VX) & (y >= 0) & (y < VY)
    bit = jnp.left_shift(1, lax.broadcasted_iota(jnp.int32, (32, 128), 0))
    words_v[...] = jnp.sum(jnp.where(inside, bit, 0), axis=0, keepdims=True)
    word_copy = pltpu.make_async_copy(words_v, words_s, word_sem)
    word_copy.start()

    def clear(l, carry):
        for p in range(VX):
            inject_ref[p, l] = jnp.zeros((VY, 128), F32)
        return carry

    lax.fori_loop(0, LT, clear, 0)
    copies[3].wait()
    stencil(ext, prev_ref, velocity_ref, partial_ref)
    for copy in copies[1:3]:
        copy.wait()
    word_copy.wait()

    def words_from(first, carry):
        words = [words_s[0, 8 * first + k] for k in range(8)]
        some = functools.reduce(lax.bitwise_or, words)

        @pl.when(some != 0)
        def _():
            for k in range(8):

                def one(bits, k=k):
                    low = bits & (-bits)
                    j = (31 - lax.clz(low)) * 128 + 8 * first + k
                    cell = cells[j]
                    add_point(partial_ref, cell, traces[0, j], velocity_ref)
                    add_point(inject_ref, cell, traces[1, j])
                    return bits & (bits - 1)

                lax.while_loop(lambda bits: bits != 0, one, words[k])

        return carry

    lax.fori_loop(0, 16, words_from, 0)


def first_source_kernel(
    now_ref,
    prev_hbm,
    velocity_hbm,
    cells_hbm,
    wavelet_hbm,
    partial_ref,
    velocity_ref,
    ext,
    prev_ref,
    cells,
    wavelet,
    sems,
):
    copies = start_all(
        ((velocity_hbm, velocity_ref), (prev_hbm, prev_ref), (cells_hbm, cells), (wavelet_hbm, wavelet)), sems
    )
    clear_ext(ext)
    fill_ext(ext, now_ref)
    for copy in copies:
        copy.wait()
    stencil(ext, prev_ref, velocity_ref, partial_ref)
    add_sources(partial_ref, cells, wavelet, 0, velocity_ref)


def source_kernel(
    fill, instant, now_ref, older_ref, velocity_ref, cells_hbm, wavelet_hbm, partial_ref, ext, cells, wavelet, sems
):
    copies = start_all(((cells_hbm, cells), (wavelet_hbm, wavelet)), sems)
    clear_ext(ext)
    fill(ext, now_ref)
    stencil(ext, older_ref, velocity_ref, partial_ref)
    for copy in copies:
        copy.wait()
    add_sources(partial_ref, cells, wavelet, instant, velocity_ref)


def second_local_kernel(
    source_ref,
    receiver_ref,
    source_old,
    receiver_old,
    velocity_ref,
    inject_ref,
    cells_hbm,
    wavelet_hbm,
    source_part,
    receiver_part,
    ext,
    cells,
    wavelet,
    sems,
):
    source_kernel(
        fill_ext_tiled, 1, source_ref, source_old, velocity_ref, cells_hbm, wavelet_hbm, source_part, ext, cells, wavelet, sems
    )
    fill_ext_tiled(ext, receiver_ref)
    stencil(ext, receiver_old, velocity_ref, receiver_part, inject_ref)


def halo_terms(m1, m2, m3, m4, rows_low, rows_high, f, l, flags):
    gx_even, has_left, has_right, gy_even, has_below, has_above = flags
    left, right = [], []
    for p in range(4):
        a, b = m1[f, p, l], m2[f, p, l]
        left.append(jnp.where(has_left, pick(gx_even, b, a), 0.0))
        right.append(jnp.where(has_right, pick(gx_even, a, b), 0.0))
    out = []
    for p in range(VX):
        i, r = p % 4, 4 * (p // 4)
        a, b = m3[f, i, l, r : r + 4, :], m4[f, i, l, r : r + 4, :]
        rows_low[p, 0:4, :] = jnp.where(has_below, pick(gy_even, b, a), 0.0)
        rows_high[p, 8:12, :] = jnp.where(has_above, pick(gy_even, a, b), 0.0)
    for p in range(VX):
        below = COEF[1] * rows_low[p, 3:11, :]
        above = COEF[1] * rows_high[p, 1:9, :]
        for d in range(2, 5):
            below = below + COEF[d] * rows_low[p, 4 - d : 12 - d, :]
            above = above + COEF[d] * rows_high[p, d : d + 8, :]
        total = jnp.concatenate((below, above), axis=0)
        for d in range(1, 5):
            if p - d < 0:
                total = total + COEF[d] * left[4 + p - d]
            if p + d >= VX:
                total = total + COEF[d] * right[p + d - VX]
        out.append(total)
    return out


def flags_of():
    gx, gy = lax.axis_index("gx"), lax.axis_index("gy")
    return (
        lax.rem(gx, 2) == 0,
        gx > 0,
        gx < lax.axis_size("gx") - 1,
        lax.rem(gy, 2) == 0,
        gy > 0,
        gy < lax.axis_size("gy") - 1,
    )


def clear_rows(rows_low, rows_high):
    for p in range(VX):
        rows_low[p] = jnp.zeros((16, 128), F32)
        rows_high[p] = jnp.zeros((16, 128), F32)


def first_halo_kernel(
    source_part,
    receiver_part,
    velocity_ref,
    m2,
    m1,
    m3,
    m4,
    source_ref,
    receiver_ref,
    s1,
    s2,
    s3,
    s4,
    coarse_ref,
    rows_low,
    rows_high,
):
    flags = flags_of()
    gx_even, gy_even = flags[0], flags[3]
    clear_rows(rows_low, rows_high)
    for f, (part, out) in enumerate(((source_part, source_ref), (receiver_part, receiver_ref))):

        def tile(l, carry, f=f, part=part, out=out):
            terms = halo_terms(m1, m2, m3, m4, rows_low, rows_high, f, l, flags)
            new = []
            for p in range(VX):
                value = part[p, l] + velocity_ref[p, :, lanes_of(l)] * terms[p]
                out[p, l] = value
                new.append(value)
            for p in range(4):
                s1[f, p, l] = pick(gx_even, new[p + 4], new[p])
                s2[f, p, l] = pick(gx_even, new[p], new[p + 4])
            pack_rows(s3, s4, f, l, [v[0:4] for v in new], [v[12:16] for v in new], gy_even)
            return carry

        lax.fori_loop(0, LT, tile, 0)
        for k in range(KT):
            low = [coarse_tile(out, (p,), k) for p in range(4)]
            high = [coarse_tile(out, (p + 4,), k) for p in range(4)]
            for p in range(4):
                coarse_ref[f, p, k] = low[p]
                coarse_ref[f, p + 4, k] = high[p]
                at = p * KT + k
                rows = slice(8 * (at % 2), 8 * (at % 2) + 8)
                s1[f, 4, at // 2, rows, :] = pick(gx_even, low[p], high[p])
                s2[f, 4, at // 2, rows, :] = pick(gx_even, high[p], low[p])


def second_halo_kernel(
    source_part,
    receiver_part,
    velocity_ref,
    m2,
    m1,
    m3,
    m4,
    source_ref,
    receiver_ref,
    coarse_ref,
    rows_low,
    rows_high,
    stage,
):
    flags = flags_of()
    clear_rows(rows_low, rows_high)
    for f, (part, out) in enumerate(((source_part, source_ref), (receiver_part, receiver_ref))):

        def tile(l, carry, f=f, part=part, out=out):
            terms = halo_terms(m1, m2, m3, m4, rows_low, rows_high, f, l, flags)
            for p in range(VX):
                value = part[p, l] + velocity_ref[p, :, lanes_of(l)] * terms[p]
                out[p, :, lanes_of(l)] = value
                stage[p, l] = value
            return carry

        lax.fori_loop(0, LT, tile, 0)
        for k in range(KT):
            for p in range(VX):
                coarse_ref[f, p, k] = coarse_tile(stage, (p,), k)


def first_image_kernel(coarse_ref, m1, m2, source_ref, receiver_ref, image_ref, source_hbm, receiver_hbm, sems):
    gx_even, has_left, has_right = flags_of()[:3]
    copies = [
        pltpu.make_async_copy(source_ref, source_hbm, sems.at[0]),
        pltpu.make_async_copy(receiver_ref, receiver_hbm, sems.at[1]),
    ]
    for copy in copies:
        copy.start()

    def planes(f, k):
        left, right = [], []
        near1 = [coarse_tile(m1, (f, p), k) for p in range(4)]
        near2 = [coarse_tile(m2, (f, p), k) for p in range(4)]
        far1, far2 = [], []
        for p in range(4):
            at = p * KT + k
            rows = slice(8 * (at % 2), 8 * (at % 2) + 8)
            far1.append(m1[f, 4, at // 2, rows, :])
            far2.append(m2[f, 4, at // 2, rows, :])
        for p in range(4):
            left.append(jnp.where(has_left, pick(gx_even, far2[p], far1[p]), 0.0))
        for p in range(4):
            left.append(jnp.where(has_left, pick(gx_even, near2[p], near1[p]), 0.0))
        for p in range(4):
            right.append(jnp.where(has_right, pick(gx_even, near1[p], near2[p]), 0.0))
        for p in range(4):
            right.append(jnp.where(has_right, pick(gx_even, far1[p], far2[p]), 0.0))
        return left + [coarse_ref[f, p, k] for p in range(VX)] + right

    for k in range(KT):
        source, receiver = planes(0, k), planes(1, k)
        for offset in range(NOFF):
            h = offset - REACH
            for a in range(VX // 2):
                image_ref[offset, a, k] = source[2 * a - h + REACH] * receiver[2 * a + h + REACH]
    for copy in copies:
        copy.wait()


def second_image_kernel(coarse_ref, m1, m2, before_ref, image_hbm, span, stage, sems):
    gx_even, has_left, has_right = flags_of()[:3]
    for f in range(2):
        for p in range(VX):
            span[f, p + REACH] = coarse_ref[f, p]
            for k in range(KT):
                a, b = m1[f, p, k], m2[f, p, k]
                span[f, p, k] = jnp.where(has_left, pick(gx_even, b, a), 0.0)
                span[f, p + REACH + VX, k] = jnp.where(has_right, pick(gx_even, a, b), 0.0)

    copies = []
    for a in range(VX // 2):
        for offset in range(NOFF):
            h = offset - REACH
            left, right = 2 * a - h + REACH, 2 * a + h + REACH
            for k in range(KT):
                value = before_ref[offset, a, k] + span[0, left, k] * span[1, right, k]
                stage[offset, a, :, k * 128 : (k + 1) * 128] = value
        copy = pltpu.make_async_copy(stage.at[:, a], image_hbm.at[:, a], sems.at[a])
        copy.start()
        copies.append(copy)
    for copy in copies:
        copy.wait()


VMEM = pl.BlockSpec(memory_space=pltpu.VMEM)
HBM = pl.BlockSpec(memory_space=pltpu.HBM)


def call(kernel, ins, outs, scratch=(), name=None, limit=12):
    return pl.pallas_call(
        kernel,
        out_shape=[jax.ShapeDtypeStruct(s, F32) for _, s in outs],
        in_specs=[s for s, _ in ins],
        out_specs=[s for s, _ in outs],
        scratch_shapes=list(scratch),
        name=name,
        cost_estimate=pl.CostEstimate(flops=0, bytes_accessed=0, transcendentals=0),
        compiler_params=pltpu.CompilerParams(vmem_limit_bytes=limit << 20),
    )(*[pltpu.with_memory_space_constraint(a, pltpu.HBM) if s is HBM else a for s, a in ins])


def vmem(*items):
    return [(VMEM, a) for a in items]


def hbm(*items):
    return [(HBM, a) for a in items]


def arrived(flops, *arrays):
    n = len(arrays)
    return pl.pallas_call(
        lambda *refs: None,
        out_shape=[jax.ShapeDtypeStruct(a.shape, F32) for a in arrays],
        in_specs=[VMEM] * n,
        out_specs=[VMEM] * n,
        input_output_aliases={i: i for i in range(n)},
        name="arrived",
        cost_estimate=pl.CostEstimate(flops=flops, bytes_accessed=0, transcendentals=0),
        compiler_params=pltpu.CompilerParams(vmem_limit_bytes=12 << 20),
    )(*arrays)


def dma(count):
    return pltpu.SemaphoreType.DMA((count,))


def inner(axis):
    return [(i, i ^ 1) for i in range(lax.axis_size(axis))]


def x_outer():
    nx, ny = lax.axis_size("gx"), lax.axis_size("gy")
    pairs = []
    for x in range(nx):
        for y in range(ny):
            other = x + 1 if x % 2 else x - 1
            if 0 <= other < nx:
                pairs.append((x * ny + y, other * ny + y))
            elif y < 2 or y >= ny - 2:
                pairs.append((x * ny + y, x * ny + (y ^ 1)))
            else:
                pairs.append((x * ny + y, other % nx * ny + y))
    return pairs


def y_outer():
    nx, ny = lax.axis_size("gx"), lax.axis_size("gy")
    pairs = []
    for x in range(nx):
        for y in range(ny):
            other = y + 1 if y % 2 else y - 1
            if 0 <= other < ny:
                pairs.append((x * ny + y, x * ny + other))
            else:
                pairs.append((x * ny + y, (x ^ 1) * ny + y))
    return pairs


def along_x(m1, m2):
    return lax.ppermute(m1, "gx", inner("gx")), lax.ppermute(m2, ("gx", "gy"), x_outer())


def inner_y(m3):
    return lax.ppermute(m3, "gy", inner("gy"))


def outer_y(m4):
    return lax.ppermute(m4, ("gx", "gy"), y_outer())


def local(
    source_now,
    source_prev,
    receiver_now,
    receiver_prev,
    velocity_sq,
    source_cells,
    source_wavelet,
    receiver_cells,
    receiver_traces,
):
    block = (VX, VY, VZ)
    ext = pltpu.VMEM((VX, LT + 2, 32, 128), F32)
    rows = pltpu.VMEM((VX, 16, 128), F32)
    whole = pltpu.VMEM(block, F32)
    m1, m2, m3, m4, source, receiver = call(
        first_pack_kernel,
        hbm(source_now, receiver_now),
        vmem(XSLAB, XSLAB, YSLAB, YSLAB, block, block),
        (dma(2),),
        name="pack",
    )
    g1, g2 = along_x(m1, m2)
    g3 = inner_y(m3)
    source_scratch = (
        ext,
        pltpu.SMEM(source_cells.shape, jnp.int32),
        pltpu.SMEM(source_wavelet.shape, F32),
        dma(2),
    )
    source_part, velocity = call(
        first_source_kernel,
        vmem(source) + hbm(source_prev, velocity_sq, source_cells, source_wavelet),
        vmem(FIELD, block),
        (
            ext,
            whole,
            pltpu.SMEM(source_cells.shape, jnp.int32),
            pltpu.SMEM(source_wavelet.shape, F32),
            dma(4),
        ),
        name="source1",
    )
    m4, source_part = lax.optimization_barrier((m4, source_part))
    g4 = outer_y(m4)
    receiver_part, inject = call(
        first_receiver_kernel,
        vmem(receiver, velocity)
        + hbm(receiver_prev, receiver_cells.reshape(32, 128), receiver_cells, receiver_traces),
        vmem(FIELD, FIELD),
        (
            ext,
            whole,
            pltpu.VMEM((32, 128), jnp.int32),
            pltpu.SMEM(receiver_cells.shape, jnp.int32),
            pltpu.SMEM(receiver_traces.shape, F32),
            pltpu.VMEM((1, 128), jnp.int32),
            pltpu.SMEM((1, 128), jnp.int32),
            dma(4),
            pltpu.SemaphoreType.DMA,
        ),
        name="receiver1",
    )
    source1, receiver1, m1, m2, m3, m4, coarse = call(
        first_halo_kernel,
        vmem(source_part, receiver_part, velocity, g2, g1, g3, g4),
        vmem(FIELD, FIELD, XSLAB_COARSE, XSLAB_COARSE, YSLAB, YSLAB, COARSE),
        (rows, rows),
        name="halo1",
    )
    g4 = outer_y(m4)
    g1, g2 = along_x(m1, m2)
    g3 = inner_y(m3)
    source_part, receiver_part = call(
        second_local_kernel,
        vmem(source1, receiver1, source, receiver, velocity, inject) + hbm(source_cells, source_wavelet),
        vmem(FIELD, FIELD),
        source_scratch,
        name="local2",
    )
    g2, g4 = arrived(4300000000, g2, g4)
    source, receiver, last = call(
        second_halo_kernel,
        vmem(source_part, receiver_part, velocity, g2, g1, g3, g4),
        vmem(block, block, COARSE),
        (rows, rows, pltpu.VMEM(FIELD, F32)),
        name="halo2",
    )
    far = along_x(last, last)
    image, source_next, receiver_next = call(
        first_image_kernel,
        vmem(coarse, g1, g2, source, receiver),
        vmem((NOFF, VX // 2, KT, 8, 128)) + hbm(block, block),
        (dma(2),),
        name="image1",
    )
    (image,) = call(
        second_image_kernel,
        vmem(last, *far, image),
        hbm((NOFF, VX // 2, 8, KT * 128)),
        (
            pltpu.VMEM((2, 2 * REACH + VX, KT, 8, 128), F32),
            pltpu.VMEM((NOFF, VX // 2, 8, KT * 128), F32),
            dma(VX // 2),
        ),
        name="image2",
    )
    return source_next, receiver_next, image


def solution(mesh):
    field = P("gx", "gy", None)
    return jax.shard_map(
        local,
        mesh=mesh,
        in_specs=(field,) * 5 + (P(),) * 4,
        out_specs=(field, field, P(None, "gx", "gy", None)),
        check_vma=False,
    )
```

```python
import functools

import jax
import jax.numpy as jnp
from jax import lax
from jax.experimental import pallas as pl
from jax.experimental.pallas import tpu as pltpu
from jax.sharding import PartitionSpec as P

COEF = (-205.0 / 72.0, 8.0 / 5.0, -1.0 / 5.0, 8.0 / 315.0, -1.0 / 560.0)
NOFF = 17
REACH = 8
VX, VY, VZ = 8, 16, 1024
LT = VZ // 128
KT = LT // 2
F32 = jnp.float32

FIELD = (VX, LT, VY, 128)
XSLAB = (2, 4, LT, VY, 128)
XSLAB_COARSE = (2, 5, LT, VY, 128)
YSLAB = (2, 4, LT, 8, 128)
COARSE = (2, VX, KT, 8, 128)


def lane_iota(shape):
    return lax.broadcasted_iota(jnp.int32, shape, len(shape) - 1)


def pick(flag, yes, no):
    return jnp.where(flag, yes, no)


def compact_even(first, second):
    lane = lane_iota((8, 128))
    index = (2 * lane) & 127
    left = jnp.take_along_axis(first, index, axis=1)
    right = jnp.take_along_axis(second, index, axis=1)
    return jnp.where(lane < 64, left, right)


def coarse_tile(ref, lead, k):
    first = ref[lead + (2 * k, pl.ds(0, 8, stride=2), slice(None))]
    second = ref[lead + (2 * k + 1, pl.ds(0, 8, stride=2), slice(None))]
    return compact_even(first, second)


def pack_rows(top_ref, bottom_ref, f, l, low, high, gy_even):
    for p in range(VX):
        i, r = p % 4, 4 * (p // 4)
        top_ref[f, i, l, r : r + 4, :] = pick(gy_even, high[p], low[p])
        bottom_ref[f, i, l, r : r + 4, :] = pick(gy_even, low[p], high[p])


def first_pack_kernel(
    source_hbm,
    receiver_hbm,
    m1,
    m2,
    m3,
    m4,
    source_ref,
    receiver_ref,
    sems,
):
    gx_even = lax.rem(lax.axis_index("gx"), 2) == 0
    gy_even = lax.rem(lax.axis_index("gy"), 2) == 0
    copies = start_all(((source_hbm, source_ref), (receiver_hbm, receiver_ref)), sems)
    for f, ref in enumerate((source_ref, receiver_ref)):
        copies[f].wait()

        def tile(l, carry, f=f, ref=ref):
            lanes = pl.ds(pl.multiple_of(l * 128, 128), 128)
            for p in range(4):
                low = ref[p, :, lanes]
                high = ref[p + 4, :, lanes]
                m1[f, p, l] = pick(gx_even, high, low)
                m2[f, p, l] = pick(gx_even, low, high)
            low = [ref[p, 0:4, lanes] for p in range(VX)]
            high = [ref[p, 12:16, lanes] for p in range(VX)]
            pack_rows(m3, m4, f, l, low, high, gy_even)
            return carry

        lax.fori_loop(0, LT, tile, 0)


def star(ext, l, lane):
    centers = [ext[p, l + 1, 8 : 8 + VY, :] for p in range(VX)]
    out = []
    for p in range(VX):
        center = centers[p]
        after = ext[p, l + 2, 8 : 8 + VY, :]
        before = ext[p, l, 8 : 8 + VY, :]
        total = (3.0 * COEF[0]) * center
        for d in range(1, 5):
            near = pltpu.roll(jnp.where(lane >= d, center, after), 128 - d, 1)
            near = near + pltpu.roll(jnp.where(lane < 128 - d, center, before), d, 1)
            near = near + ext[p, l + 1, 8 + d : 8 + d + VY, :]
            near = near + ext[p, l + 1, 8 - d : 8 - d + VY, :]
            if p + d < VX:
                near = near + centers[p + d]
            if p - d >= 0:
                near = near + centers[p - d]
            total = total + COEF[d] * near
        out.append(total)
    return centers, out


def clear_ext(ext):
    def tile(p, carry):
        ext[p, :, 0:8, :] = jnp.zeros((LT + 2, 8, 128), F32)
        ext[p, :, 24:32, :] = jnp.zeros((LT + 2, 8, 128), F32)
        for l in (0, LT + 1):
            ext[p, l, 8:24, :] = jnp.zeros((VY, 128), F32)
        return carry

    lax.fori_loop(0, VX, tile, 0)


def lanes_of(l):
    return pl.ds(pl.multiple_of(l * 128, 128), 128)


def locate(cell):
    x = lax.shift_right_logical(cell, 17) - lax.axis_index("gx") * VX
    y = (lax.shift_right_logical(cell, 10) & 127) - lax.axis_index("gy") * VY
    return x, y, cell & 1023


def add_point(ref, cell, amount, velocity_ref=None):
    x, y, z = locate(cell)
    l = lax.shift_right_logical(z, 7)
    value = jnp.full((VY, 128), amount, F32)
    if velocity_ref is not None:
        value = value * velocity_ref[x, :, lanes_of(l)]
    row = lax.broadcasted_iota(jnp.int32, (VY, 128), 0)
    here = (row == y) & (lane_iota((VY, 128)) == (z & 127))
    ref[x, l] = ref[x, l] + jnp.where(here, value, 0.0)


def add_sources(ref, cells, wavelet, instant, velocity_ref):
    for j in range(cells.shape[0]):
        cell = cells[j]
        x, y, _ = locate(cell)
        here = (x >= 0) & (x < VX) & (y >= 0) & (y < VY)

        @pl.when(here)
        def _(cell=cell, j=j):
            add_point(ref, cell, wavelet[instant, j], velocity_ref)


def stencil(ext, older, velocity_ref, partial_ref, inject_ref=None):
    lane = lane_iota((VY, 128))

    def tile(l, carry):
        centers, totals = star(ext, l, lane)
        for p in range(VX):
            total = totals[p]
            if inject_ref is not None:
                total = total + inject_ref[p, l]
            v = velocity_ref[p, :, lanes_of(l)]
            partial_ref[p, l] = (2.0 * centers[p] - older[p, :, lanes_of(l)]) + v * total
        return carry

    lax.fori_loop(0, LT, tile, 0)


def start_all(pairs, sems):
    copies = [pltpu.make_async_copy(a, b, sems.at[i]) for i, (a, b) in enumerate(pairs)]
    for copy in copies:
        copy.start()
    return copies


def fill_ext(ext, ref):
    def tile(l, carry):
        for p in range(VX):
            ext[p, l + 1, 8 : 8 + VY, :] = ref[p, :, lanes_of(l)]
        return carry

    lax.fori_loop(0, LT, tile, 0)


def fill_ext_tiled(ext, ref):
    def tile(l, carry):
        for p in range(VX):
            ext[p, l + 1, 8 : 8 + VY, :] = ref[p, l]
        return carry

    lax.fori_loop(0, LT, tile, 0)


def first_receiver_kernel(
    now_ref,
    velocity_ref,
    prev_hbm,
    grid_hbm,
    cells_hbm,
    traces_hbm,
    partial_ref,
    inject_ref,
    ext,
    prev_ref,
    grid_ref,
    cells,
    traces,
    words_v,
    words_s,
    sems,
    word_sem,
):
    copies = start_all(
        ((grid_hbm, grid_ref), (cells_hbm, cells), (traces_hbm, traces), (prev_hbm, prev_ref)), sems
    )
    clear_ext(ext)
    fill_ext(ext, now_ref)

    copies[0].wait()
    x, y, _ = locate(grid_ref[...])
    inside = (x >= 0) & (x < VX) & (y >= 0) & (y < VY)
    bit = jnp.left_shift(1, lax.broadcasted_iota(jnp.int32, (32, 128), 0))
    words_v[...] = jnp.sum(jnp.where(inside, bit, 0), axis=0, keepdims=True)
    word_copy = pltpu.make_async_copy(words_v, words_s, word_sem)
    word_copy.start()

    def clear(l, carry):
        for p in range(VX):
            inject_ref[p, l] = jnp.zeros((VY, 128), F32)
        return carry

    lax.fori_loop(0, LT, clear, 0)
    copies[3].wait()
    stencil(ext, prev_ref, velocity_ref, partial_ref)
    for copy in copies[1:3]:
        copy.wait()
    word_copy.wait()

    def words_from(first, carry):
        words = [words_s[0, 8 * first + k] for k in range(8)]
        some = functools.reduce(lax.bitwise_or, words)

        @pl.when(some != 0)
        def _():
            for k in range(8):

                def one(bits, k=k):
                    low = bits & (-bits)
                    j = (31 - lax.clz(low)) * 128 + 8 * first + k
                    cell = cells[j]
                    add_point(partial_ref, cell, traces[0, j], velocity_ref)
                    add_point(inject_ref, cell, traces[1, j])
                    return bits & (bits - 1)

                lax.while_loop(lambda bits: bits != 0, one, words[k])

        return carry

    lax.fori_loop(0, 16, words_from, 0)


def first_source_kernel(
    now_ref,
    prev_hbm,
    velocity_hbm,
    cells_hbm,
    wavelet_hbm,
    partial_ref,
    velocity_ref,
    ext,
    prev_ref,
    cells,
    wavelet,
    sems,
):
    copies = start_all(
        ((velocity_hbm, velocity_ref), (prev_hbm, prev_ref), (cells_hbm, cells), (wavelet_hbm, wavelet)), sems
    )
    clear_ext(ext)
    fill_ext(ext, now_ref)
    for copy in copies:
        copy.wait()
    stencil(ext, prev_ref, velocity_ref, partial_ref)
    add_sources(partial_ref, cells, wavelet, 0, velocity_ref)


def source_kernel(
    fill, instant, now_ref, older_ref, velocity_ref, cells_hbm, wavelet_hbm, partial_ref, ext, cells, wavelet, sems
):
    copies = start_all(((cells_hbm, cells), (wavelet_hbm, wavelet)), sems)
    clear_ext(ext)
    fill(ext, now_ref)
    stencil(ext, older_ref, velocity_ref, partial_ref)
    for copy in copies:
        copy.wait()
    add_sources(partial_ref, cells, wavelet, instant, velocity_ref)


def second_local_kernel(
    source_ref,
    receiver_ref,
    source_old,
    receiver_old,
    velocity_ref,
    inject_ref,
    cells_hbm,
    wavelet_hbm,
    source_part,
    receiver_part,
    ext,
    cells,
    wavelet,
    sems,
):
    source_kernel(
        fill_ext_tiled, 1, source_ref, source_old, velocity_ref, cells_hbm, wavelet_hbm, source_part, ext, cells, wavelet, sems
    )
    fill_ext_tiled(ext, receiver_ref)
    stencil(ext, receiver_old, velocity_ref, receiver_part, inject_ref)


def halo_terms(m1, m2, m3, m4, rows_low, rows_high, f, l, flags):
    gx_even, has_left, has_right, gy_even, has_below, has_above = flags
    left, right = [], []
    for p in range(4):
        a, b = m1[f, p, l], m2[f, p, l]
        left.append(jnp.where(has_left, pick(gx_even, b, a), 0.0))
        right.append(jnp.where(has_right, pick(gx_even, a, b), 0.0))
    out = []
    for p in range(VX):
        i, r = p % 4, 4 * (p // 4)
        a, b = m3[f, i, l, r : r + 4, :], m4[f, i, l, r : r + 4, :]
        rows_low[p, 0:4, :] = jnp.where(has_below, pick(gy_even, b, a), 0.0)
        rows_high[p, 8:12, :] = jnp.where(has_above, pick(gy_even, a, b), 0.0)
    for p in range(VX):
        below = COEF[1] * rows_low[p, 3:11, :]
        above = COEF[1] * rows_high[p, 1:9, :]
        for d in range(2, 5):
            below = below + COEF[d] * rows_low[p, 4 - d : 12 - d, :]
            above = above + COEF[d] * rows_high[p, d : d + 8, :]
        total = jnp.concatenate((below, above), axis=0)
        for d in range(1, 5):
            if p - d < 0:
                total = total + COEF[d] * left[4 + p - d]
            if p + d >= VX:
                total = total + COEF[d] * right[p + d - VX]
        out.append(total)
    return out


def flags_of():
    gx, gy = lax.axis_index("gx"), lax.axis_index("gy")
    return (
        lax.rem(gx, 2) == 0,
        gx > 0,
        gx < lax.axis_size("gx") - 1,
        lax.rem(gy, 2) == 0,
        gy > 0,
        gy < lax.axis_size("gy") - 1,
    )


def clear_rows(rows_low, rows_high):
    for p in range(VX):
        rows_low[p] = jnp.zeros((16, 128), F32)
        rows_high[p] = jnp.zeros((16, 128), F32)


def first_halo_kernel(
    source_part,
    receiver_part,
    velocity_ref,
    m2,
    m1,
    m3,
    m4,
    source_ref,
    receiver_ref,
    s1,
    s2,
    s3,
    s4,
    coarse_ref,
    rows_low,
    rows_high,
):
    flags = flags_of()
    gx_even, gy_even = flags[0], flags[3]
    clear_rows(rows_low, rows_high)
    for f, (part, out) in enumerate(((source_part, source_ref), (receiver_part, receiver_ref))):

        def tile(l, carry, f=f, part=part, out=out):
            terms = halo_terms(m1, m2, m3, m4, rows_low, rows_high, f, l, flags)
            new = []
            for p in range(VX):
                value = part[p, l] + velocity_ref[p, :, lanes_of(l)] * terms[p]
                out[p, l] = value
                new.append(value)
            for p in range(4):
                s1[f, p, l] = pick(gx_even, new[p + 4], new[p])
                s2[f, p, l] = pick(gx_even, new[p], new[p + 4])
            pack_rows(s3, s4, f, l, [v[0:4] for v in new], [v[12:16] for v in new], gy_even)
            return carry

        lax.fori_loop(0, LT, tile, 0)
        for k in range(KT):
            low = [coarse_tile(out, (p,), k) for p in range(4)]
            high = [coarse_tile(out, (p + 4,), k) for p in range(4)]
            for p in range(4):
                coarse_ref[f, p, k] = low[p]
                coarse_ref[f, p + 4, k] = high[p]
                at = p * KT + k
                rows = slice(8 * (at % 2), 8 * (at % 2) + 8)
                s1[f, 4, at // 2, rows, :] = pick(gx_even, low[p], high[p])
                s2[f, 4, at // 2, rows, :] = pick(gx_even, high[p], low[p])


def second_halo_kernel(
    source_part,
    receiver_part,
    velocity_ref,
    m2,
    m1,
    m3,
    m4,
    source_ref,
    receiver_ref,
    coarse_ref,
    rows_low,
    rows_high,
    stage,
):
    flags = flags_of()
    clear_rows(rows_low, rows_high)
    for f, (part, out) in enumerate(((source_part, source_ref), (receiver_part, receiver_ref))):

        def tile(l, carry, f=f, part=part, out=out):
            terms = halo_terms(m1, m2, m3, m4, rows_low, rows_high, f, l, flags)
            for p in range(VX):
                value = part[p, l] + velocity_ref[p, :, lanes_of(l)] * terms[p]
                out[p, :, lanes_of(l)] = value
                stage[p, l] = value
            return carry

        lax.fori_loop(0, LT, tile, 0)
        for k in range(KT):
            for p in range(VX):
                coarse_ref[f, p, k] = coarse_tile(stage, (p,), k)


def first_image_kernel(coarse_ref, m1, m2, source_ref, receiver_ref, image_ref, source_hbm, receiver_hbm, sems):
    gx_even, has_left, has_right = flags_of()[:3]
    copies = [
        pltpu.make_async_copy(source_ref, source_hbm, sems.at[0]),
        pltpu.make_async_copy(receiver_ref, receiver_hbm, sems.at[1]),
    ]
    for copy in copies:
        copy.start()

    def planes(f, k):
        left, right = [], []
        near1 = [coarse_tile(m1, (f, p), k) for p in range(4)]
        near2 = [coarse_tile(m2, (f, p), k) for p in range(4)]
        far1, far2 = [], []
        for p in range(4):
            at = p * KT + k
            rows = slice(8 * (at % 2), 8 * (at % 2) + 8)
            far1.append(m1[f, 4, at // 2, rows, :])
            far2.append(m2[f, 4, at // 2, rows, :])
        for p in range(4):
            left.append(jnp.where(has_left, pick(gx_even, far2[p], far1[p]), 0.0))
        for p in range(4):
            left.append(jnp.where(has_left, pick(gx_even, near2[p], near1[p]), 0.0))
        for p in range(4):
            right.append(jnp.where(has_right, pick(gx_even, near1[p], near2[p]), 0.0))
        for p in range(4):
            right.append(jnp.where(has_right, pick(gx_even, far1[p], far2[p]), 0.0))
        return left + [coarse_ref[f, p, k] for p in range(VX)] + right

    for k in range(KT):
        source, receiver = planes(0, k), planes(1, k)
        for offset in range(NOFF):
            h = offset - REACH
            for a in range(VX // 2):
                image_ref[offset, a, k] = source[2 * a - h + REACH] * receiver[2 * a + h + REACH]
    for copy in copies:
        copy.wait()


def second_image_kernel(coarse_ref, m1, m2, before_ref, image_hbm, span, stage, sems):
    gx_even, has_left, has_right = flags_of()[:3]
    for f in range(2):
        for p in range(VX):
            span[f, p + REACH] = coarse_ref[f, p]
            for k in range(KT):
                a, b = m1[f, p, k], m2[f, p, k]
                span[f, p, k] = jnp.where(has_left, pick(gx_even, b, a), 0.0)
                span[f, p + REACH + VX, k] = jnp.where(has_right, pick(gx_even, a, b), 0.0)

    copies = []
    for a in range(VX // 2):
        for offset in range(NOFF):
            h = offset - REACH
            left, right = 2 * a - h + REACH, 2 * a + h + REACH
            for k in range(KT):
                value = before_ref[offset, a, k] + span[0, left, k] * span[1, right, k]
                stage[offset, a, :, k * 128 : (k + 1) * 128] = value
        copy = pltpu.make_async_copy(stage.at[:, a], image_hbm.at[:, a], sems.at[a])
        copy.start()
        copies.append(copy)
    for copy in copies:
        copy.wait()


VMEM = pl.BlockSpec(memory_space=pltpu.VMEM)
HBM = pl.BlockSpec(memory_space=pltpu.HBM)


def call(kernel, ins, outs, scratch=(), name=None, limit=12):
    return pl.pallas_call(
        kernel,
        out_shape=[jax.ShapeDtypeStruct(s, F32) for _, s in outs],
        in_specs=[s for s, _ in ins],
        out_specs=[s for s, _ in outs],
        scratch_shapes=list(scratch),
        name=name,
        cost_estimate=pl.CostEstimate(flops=0, bytes_accessed=0, transcendentals=0),
        compiler_params=pltpu.CompilerParams(vmem_limit_bytes=limit << 20),
    )(*[pltpu.with_memory_space_constraint(a, pltpu.HBM) if s is HBM else a for s, a in ins])


def vmem(*items):
    return [(VMEM, a) for a in items]


def hbm(*items):
    return [(HBM, a) for a in items]


def arrived(flops, *arrays):
    n = len(arrays)
    return pl.pallas_call(
        lambda *refs: None,
        out_shape=[jax.ShapeDtypeStruct(a.shape, F32) for a in arrays],
        in_specs=[VMEM] * n,
        out_specs=[VMEM] * n,
        input_output_aliases={i: i for i in range(n)},
        name="arrived",
        cost_estimate=pl.CostEstimate(flops=flops, bytes_accessed=0, transcendentals=0),
        compiler_params=pltpu.CompilerParams(vmem_limit_bytes=12 << 20),
    )(*arrays)


def dma(count):
    return pltpu.SemaphoreType.DMA((count,))


def inner(axis):
    return [(i, i ^ 1) for i in range(lax.axis_size(axis))]


def x_outer(near):
    nx, ny = lax.axis_size("gx"), lax.axis_size("gy")
    pairs = []
    for x in range(nx):
        for y in range(ny):
            other = x + 1 if x % 2 else x - 1
            if 0 <= other < nx:
                pairs.append((x * ny + y, other * ny + y))
            elif min(y, ny - 1 - y) < near:
                pairs.append((x * ny + y, x * ny + (y ^ 1)))
            else:
                pairs.append((x * ny + y, other % nx * ny + y))
    return pairs


def y_outer():
    nx, ny = lax.axis_size("gx"), lax.axis_size("gy")
    pairs = []
    for x in range(nx):
        for y in range(ny):
            other = y + 1 if y % 2 else y - 1
            if 0 <= other < ny:
                pairs.append((x * ny + y, x * ny + other))
            else:
                pairs.append((x * ny + y, (x ^ 1) * ny + y))
    return pairs


def along_x(m1, m2, near=4):
    return lax.ppermute(m1, "gx", inner("gx")), lax.ppermute(m2, ("gx", "gy"), x_outer(near))


def inner_y(m3):
    return lax.ppermute(m3, "gy", inner("gy"))


def outer_y(m4):
    return lax.ppermute(m4, ("gx", "gy"), y_outer())


def local(
    source_now,
    source_prev,
    receiver_now,
    receiver_prev,
    velocity_sq,
    source_cells,
    source_wavelet,
    receiver_cells,
    receiver_traces,
):
    block = (VX, VY, VZ)
    ext = pltpu.VMEM((VX, LT + 2, 32, 128), F32)
    rows = pltpu.VMEM((VX, 16, 128), F32)
    whole = pltpu.VMEM(block, F32)
    m1, m2, m3, m4, source, receiver = call(
        first_pack_kernel,
        hbm(source_now, receiver_now),
        vmem(XSLAB, XSLAB, YSLAB, YSLAB, block, block),
        (dma(2),),
        name="pack",
    )
    g1, g2 = along_x(m1, m2)
    g3 = inner_y(m3)
    source_scratch = (
        ext,
        pltpu.SMEM(source_cells.shape, jnp.int32),
        pltpu.SMEM(source_wavelet.shape, F32),
        dma(2),
    )
    source_part, velocity = call(
        first_source_kernel,
        vmem(source) + hbm(source_prev, velocity_sq, source_cells, source_wavelet),
        vmem(FIELD, block),
        (
            ext,
            whole,
            pltpu.SMEM(source_cells.shape, jnp.int32),
            pltpu.SMEM(source_wavelet.shape, F32),
            dma(4),
        ),
        name="source1",
    )
    m4, source_part = lax.optimization_barrier((m4, source_part))
    g4 = outer_y(m4)
    receiver_part, inject = call(
        first_receiver_kernel,
        vmem(receiver, velocity)
        + hbm(receiver_prev, receiver_cells.reshape(32, 128), receiver_cells, receiver_traces),
        vmem(FIELD, FIELD),
        (
            ext,
            whole,
            pltpu.VMEM((32, 128), jnp.int32),
            pltpu.SMEM(receiver_cells.shape, jnp.int32),
            pltpu.SMEM(receiver_traces.shape, F32),
            pltpu.VMEM((1, 128), jnp.int32),
            pltpu.SMEM((1, 128), jnp.int32),
            dma(4),
            pltpu.SemaphoreType.DMA,
        ),
        name="receiver1",
    )
    source1, receiver1, m1, m2, m3, m4, coarse = call(
        first_halo_kernel,
        vmem(source_part, receiver_part, velocity, g2, g1, g3, g4),
        vmem(FIELD, FIELD, XSLAB_COARSE, XSLAB_COARSE, YSLAB, YSLAB, COARSE),
        (rows, rows),
        name="halo1",
    )
    g4 = outer_y(m4)
    g1, g2 = along_x(m1, m2, near=2)
    g3 = inner_y(m3)
    source_part, receiver_part = call(
        second_local_kernel,
        vmem(source1, receiver1, source, receiver, velocity, inject) + hbm(source_cells, source_wavelet),
        vmem(FIELD, FIELD),
        source_scratch,
        name="local2",
    )
    g2, g4 = arrived(4300000000, g2, g4)
    source, receiver, last = call(
        second_halo_kernel,
        vmem(source_part, receiver_part, velocity, g2, g1, g3, g4),
        vmem(block, block, COARSE),
        (rows, rows, pltpu.VMEM(FIELD, F32)),
        name="halo2",
    )
    far = along_x(last, last)
    image, source_next, receiver_next = call(
        first_image_kernel,
        vmem(coarse, g1, g2, source, receiver),
        vmem((NOFF, VX // 2, KT, 8, 128)) + hbm(block, block),
        (dma(2),),
        name="image1",
    )
    (image,) = call(
        second_image_kernel,
        vmem(last, *far, image),
        hbm((NOFF, VX // 2, 8, KT * 128)),
        (
            pltpu.VMEM((2, 2 * REACH + VX, KT, 8, 128), F32),
            pltpu.VMEM((NOFF, VX // 2, 8, KT * 128), F32),
            dma(VX // 2),
        ),
        name="image2",
    )
    return source_next, receiver_next, image


def solution(mesh):
    field = P("gx", "gy", None)
    return jax.shard_map(
        local,
        mesh=mesh,
        in_specs=(field,) * 5 + (P(),) * 4,
        out_specs=(field, field, P(None, "gx", "gy", None)),
        check_vma=False,
    )
```

```python
import functools

import jax
import jax.numpy as jnp
from jax import lax
from jax.experimental import pallas as pl
from jax.experimental.pallas import tpu as pltpu
from jax.sharding import PartitionSpec as P

COEF = (-205.0 / 72.0, 8.0 / 5.0, -1.0 / 5.0, 8.0 / 315.0, -1.0 / 560.0)
NOFF = 17
REACH = 8
VX, VY, VZ = 8, 16, 1024
LT = VZ // 128
KT = LT // 2
F32 = jnp.float32

FIELD = (VX, LT, VY, 128)
XSLAB = (2, 4, LT, VY, 128)
XSLAB_COARSE = (2, 5, LT, VY, 128)
YSLAB = (2, 4, LT, 8, 128)
COARSE = (2, VX, KT, 8, 128)


def lane_iota(shape):
    return lax.broadcasted_iota(jnp.int32, shape, len(shape) - 1)


def pick(flag, yes, no):
    return jnp.where(flag, yes, no)


def compact_even(first, second):
    lane = lane_iota((8, 128))
    index = (2 * lane) & 127
    left = jnp.take_along_axis(first, index, axis=1)
    right = jnp.take_along_axis(second, index, axis=1)
    return jnp.where(lane < 64, left, right)


def coarse_tile(ref, lead, k):
    first = ref[lead + (2 * k, pl.ds(0, 8, stride=2), slice(None))]
    second = ref[lead + (2 * k + 1, pl.ds(0, 8, stride=2), slice(None))]
    return compact_even(first, second)


def pack_rows(top_ref, bottom_ref, f, l, low, high, gy_even):
    for p in range(VX):
        i, r = p % 4, 4 * (p // 4)
        top_ref[f, i, l, r : r + 4, :] = pick(gy_even, high[p], low[p])
        bottom_ref[f, i, l, r : r + 4, :] = pick(gy_even, low[p], high[p])


def first_pack_kernel(
    source_hbm,
    receiver_hbm,
    m1,
    m2,
    m3,
    m4,
    source_ref,
    receiver_ref,
    sems,
):
    gx_even = lax.rem(lax.axis_index("gx"), 2) == 0
    gy_even = lax.rem(lax.axis_index("gy"), 2) == 0
    copies = start_all(((source_hbm, source_ref), (receiver_hbm, receiver_ref)), sems)
    for f, ref in enumerate((source_ref, receiver_ref)):
        copies[f].wait()

        def tile(l, carry, f=f, ref=ref):
            lanes = pl.ds(pl.multiple_of(l * 128, 128), 128)
            for p in range(4):
                low = ref[p, :, lanes]
                high = ref[p + 4, :, lanes]
                m1[f, p, l] = pick(gx_even, high, low)
                m2[f, p, l] = pick(gx_even, low, high)
            low = [ref[p, 0:4, lanes] for p in range(VX)]
            high = [ref[p, 12:16, lanes] for p in range(VX)]
            pack_rows(m3, m4, f, l, low, high, gy_even)
            return carry

        lax.fori_loop(0, LT, tile, 0)


def star(ext, l, lane):
    centers = [ext[p, l + 1, 8 : 8 + VY, :] for p in range(VX)]
    out = []
    for p in range(VX):
        center = centers[p]
        after = ext[p, l + 2, 8 : 8 + VY, :]
        before = ext[p, l, 8 : 8 + VY, :]
        total = (3.0 * COEF[0]) * center
        for d in range(1, 5):
            near = pltpu.roll(jnp.where(lane >= d, center, after), 128 - d, 1)
            near = near + pltpu.roll(jnp.where(lane < 128 - d, center, before), d, 1)
            near = near + ext[p, l + 1, 8 + d : 8 + d + VY, :]
            near = near + ext[p, l + 1, 8 - d : 8 - d + VY, :]
            if p + d < VX:
                near = near + centers[p + d]
            if p - d >= 0:
                near = near + centers[p - d]
            total = total + COEF[d] * near
        out.append(total)
    return centers, out


def clear_ext(ext):
    def tile(p, carry):
        ext[p, :, 0:8, :] = jnp.zeros((LT + 2, 8, 128), F32)
        ext[p, :, 24:32, :] = jnp.zeros((LT + 2, 8, 128), F32)
        for l in (0, LT + 1):
            ext[p, l, 8:24, :] = jnp.zeros((VY, 128), F32)
        return carry

    lax.fori_loop(0, VX, tile, 0)


def lanes_of(l):
    return pl.ds(pl.multiple_of(l * 128, 128), 128)


def locate(cell):
    x = lax.shift_right_logical(cell, 17) - lax.axis_index("gx") * VX
    y = (lax.shift_right_logical(cell, 10) & 127) - lax.axis_index("gy") * VY
    return x, y, cell & 1023


def add_point(ref, cell, amount, velocity_ref=None):
    x, y, z = locate(cell)
    l = lax.shift_right_logical(z, 7)
    value = jnp.full((VY, 128), amount, F32)
    if velocity_ref is not None:
        value = value * velocity_ref[x, :, lanes_of(l)]
    row = lax.broadcasted_iota(jnp.int32, (VY, 128), 0)
    here = (row == y) & (lane_iota((VY, 128)) == (z & 127))
    ref[x, l] = ref[x, l] + jnp.where(here, value, 0.0)


def add_sources(ref, cells, wavelet, instant, velocity_ref):
    for j in range(cells.shape[0]):
        cell = cells[j]
        x, y, _ = locate(cell)
        here = (x >= 0) & (x < VX) & (y >= 0) & (y < VY)

        @pl.when(here)
        def _(cell=cell, j=j):
            add_point(ref, cell, wavelet[instant, j], velocity_ref)


def stencil(ext, older, velocity_ref, partial_ref, inject_ref=None):
    lane = lane_iota((VY, 128))

    def tile(l, carry):
        centers, totals = star(ext, l, lane)
        for p in range(VX):
            total = totals[p]
            if inject_ref is not None:
                total = total + inject_ref[p, l]
            v = velocity_ref[p, :, lanes_of(l)]
            partial_ref[p, l] = (2.0 * centers[p] - older[p, :, lanes_of(l)]) + v * total
        return carry

    lax.fori_loop(0, LT, tile, 0)


def start_all(pairs, sems):
    copies = [pltpu.make_async_copy(a, b, sems.at[i]) for i, (a, b) in enumerate(pairs)]
    for copy in copies:
        copy.start()
    return copies


def fill_ext(ext, ref):
    def tile(l, carry):
        for p in range(VX):
            ext[p, l + 1, 8 : 8 + VY, :] = ref[p, :, lanes_of(l)]
        return carry

    lax.fori_loop(0, LT, tile, 0)


def fill_ext_tiled(ext, ref):
    def tile(l, carry):
        for p in range(VX):
            ext[p, l + 1, 8 : 8 + VY, :] = ref[p, l]
        return carry

    lax.fori_loop(0, LT, tile, 0)


def first_receiver_kernel(
    now_ref,
    velocity_ref,
    prev_hbm,
    grid_hbm,
    cells_hbm,
    traces_hbm,
    partial_ref,
    inject_ref,
    ext,
    prev_ref,
    grid_ref,
    cells,
    traces,
    words_v,
    words_s,
    sems,
    word_sem,
):
    copies = start_all(
        ((grid_hbm, grid_ref), (cells_hbm, cells), (traces_hbm, traces), (prev_hbm, prev_ref)), sems
    )
    clear_ext(ext)
    fill_ext(ext, now_ref)

    copies[0].wait()
    x, y, _ = locate(grid_ref[...])
    inside = (x >= 0) & (x < VX) & (y >= 0) & (y < VY)
    bit = jnp.left_shift(1, lax.broadcasted_iota(jnp.int32, (32, 128), 0))
    words_v[...] = jnp.sum(jnp.where(inside, bit, 0), axis=0, keepdims=True)
    word_copy = pltpu.make_async_copy(words_v, words_s, word_sem)
    word_copy.start()

    def clear(l, carry):
        for p in range(VX):
            inject_ref[p, l] = jnp.zeros((VY, 128), F32)
        return carry

    lax.fori_loop(0, LT, clear, 0)
    copies[3].wait()
    stencil(ext, prev_ref, velocity_ref, partial_ref)
    for copy in copies[1:3]:
        copy.wait()
    word_copy.wait()

    def words_from(first, carry):
        words = [words_s[0, 8 * first + k] for k in range(8)]
        some = functools.reduce(lax.bitwise_or, words)

        @pl.when(some != 0)
        def _():
            for k in range(8):

                def one(bits, k=k):
                    low = bits & (-bits)
                    j = (31 - lax.clz(low)) * 128 + 8 * first + k
                    cell = cells[j]
                    add_point(partial_ref, cell, traces[0, j], velocity_ref)
                    add_point(inject_ref, cell, traces[1, j])
                    return bits & (bits - 1)

                lax.while_loop(lambda bits: bits != 0, one, words[k])

        return carry

    lax.fori_loop(0, 16, words_from, 0)


def first_source_kernel(
    now_ref,
    prev_hbm,
    velocity_hbm,
    cells_hbm,
    wavelet_hbm,
    partial_ref,
    velocity_ref,
    ext,
    prev_ref,
    cells,
    wavelet,
    sems,
):
    copies = start_all(
        ((velocity_hbm, velocity_ref), (prev_hbm, prev_ref), (cells_hbm, cells), (wavelet_hbm, wavelet)), sems
    )
    clear_ext(ext)
    fill_ext(ext, now_ref)
    for copy in copies:
        copy.wait()
    stencil(ext, prev_ref, velocity_ref, partial_ref)
    add_sources(partial_ref, cells, wavelet, 0, velocity_ref)


def source_kernel(
    fill, instant, now_ref, older_ref, velocity_ref, cells_hbm, wavelet_hbm, partial_ref, ext, cells, wavelet, sems
):
    copies = start_all(((cells_hbm, cells), (wavelet_hbm, wavelet)), sems)
    clear_ext(ext)
    fill(ext, now_ref)
    stencil(ext, older_ref, velocity_ref, partial_ref)
    for copy in copies:
        copy.wait()
    add_sources(partial_ref, cells, wavelet, instant, velocity_ref)


def second_local_kernel(
    source_ref,
    receiver_ref,
    source_old,
    receiver_old,
    velocity_ref,
    inject_ref,
    cells_hbm,
    wavelet_hbm,
    source_part,
    receiver_part,
    ext,
    cells,
    wavelet,
    sems,
):
    source_kernel(
        fill_ext_tiled, 1, source_ref, source_old, velocity_ref, cells_hbm, wavelet_hbm, source_part, ext, cells, wavelet, sems
    )
    fill_ext_tiled(ext, receiver_ref)
    stencil(ext, receiver_old, velocity_ref, receiver_part, inject_ref)


def halo_terms(m1, m2, m3, m4, f, l, flags):
    gx_even, has_left, has_right, gy_even, has_below, has_above = flags
    left, right = [], []
    for p in range(4):
        a, b = m1[f, p, l], m2[f, p, l]
        left.append(jnp.where(has_left, pick(gx_even, b, a), 0.0))
        right.append(jnp.where(has_right, pick(gx_even, a, b), 0.0))
    row = lax.broadcasted_iota(jnp.int32, (8, 128), 0)
    step = row & 3
    first = row < 4
    lows, highs = [None] * VX, [None] * VX
    for i in range(4):
        a, b = m3[f, i, l], m4[f, i, l]
        low = jnp.where(has_below, pick(gy_even, b, a), 0.0)
        high = jnp.where(has_above, pick(gy_even, a, b), 0.0)
        below, above = COEF[4] * low, COEF[4] * high
        for d in range(1, 4):
            below = below + jnp.where(step < d, COEF[d], 0.0) * pltpu.roll(low, 4 + d, 0)
            above = above + jnp.where(step >= 4 - d, COEF[d], 0.0) * pltpu.roll(high, 4 - d, 0)
        lows[i] = jnp.where(first, below, 0.0)
        lows[i + 4] = jnp.where(first, pltpu.roll(below, 4, 0), 0.0)
        highs[i] = jnp.where(first, 0.0, pltpu.roll(above, 4, 0))
        highs[i + 4] = jnp.where(first, 0.0, above)
    out = []
    for p in range(VX):
        total = jnp.concatenate((lows[p], highs[p]), axis=0)
        for d in range(1, 5):
            if p - d < 0:
                total = total + COEF[d] * left[4 + p - d]
            if p + d >= VX:
                total = total + COEF[d] * right[p + d - VX]
        out.append(total)
    return out


def flags_of():
    gx, gy = lax.axis_index("gx"), lax.axis_index("gy")
    return (
        lax.rem(gx, 2) == 0,
        gx > 0,
        gx < lax.axis_size("gx") - 1,
        lax.rem(gy, 2) == 0,
        gy > 0,
        gy < lax.axis_size("gy") - 1,
    )


def first_halo_kernel(
    source_part,
    receiver_part,
    velocity_ref,
    m2,
    m1,
    m3,
    m4,
    source_ref,
    receiver_ref,
    s1,
    s2,
    s3,
    s4,
    coarse_ref,
):
    flags = flags_of()
    gx_even, gy_even = flags[0], flags[3]
    for f, (part, out) in enumerate(((source_part, source_ref), (receiver_part, receiver_ref))):

        def tile(l, carry, f=f, part=part, out=out):
            terms = halo_terms(m1, m2, m3, m4, f, l, flags)
            new = []
            for p in range(VX):
                value = part[p, l] + velocity_ref[p, :, lanes_of(l)] * terms[p]
                out[p, l] = value
                new.append(value)
            for p in range(4):
                s1[f, p, l] = pick(gx_even, new[p + 4], new[p])
                s2[f, p, l] = pick(gx_even, new[p], new[p + 4])
            pack_rows(s3, s4, f, l, [v[0:4] for v in new], [v[12:16] for v in new], gy_even)
            return carry

        lax.fori_loop(0, LT, tile, 0)
        for k in range(KT):
            low = [coarse_tile(out, (p,), k) for p in range(4)]
            high = [coarse_tile(out, (p + 4,), k) for p in range(4)]
            for p in range(4):
                coarse_ref[f, p, k] = low[p]
                coarse_ref[f, p + 4, k] = high[p]
                at = p * KT + k
                rows = slice(8 * (at % 2), 8 * (at % 2) + 8)
                s1[f, 4, at // 2, rows, :] = pick(gx_even, low[p], high[p])
                s2[f, 4, at // 2, rows, :] = pick(gx_even, high[p], low[p])


def second_halo_kernel(
    source_part,
    receiver_part,
    velocity_ref,
    m2,
    m1,
    m3,
    m4,
    source_ref,
    receiver_ref,
    coarse_ref,
    stage,
):
    flags = flags_of()
    for f, (part, out) in enumerate(((source_part, source_ref), (receiver_part, receiver_ref))):

        def tile(l, carry, f=f, part=part, out=out):
            terms = halo_terms(m1, m2, m3, m4, f, l, flags)
            for p in range(VX):
                value = part[p, l] + velocity_ref[p, :, lanes_of(l)] * terms[p]
                out[p, :, lanes_of(l)] = value
                stage[p, l] = value
            return carry

        lax.fori_loop(0, LT, tile, 0)
        for k in range(KT):
            for p in range(VX):
                coarse_ref[f, p, k] = coarse_tile(stage, (p,), k)


def first_image_kernel(coarse_ref, m1, m2, source_ref, receiver_ref, image_ref, source_hbm, receiver_hbm, sems):
    gx_even, has_left, has_right = flags_of()[:3]
    copies = [
        pltpu.make_async_copy(source_ref, source_hbm, sems.at[0]),
        pltpu.make_async_copy(receiver_ref, receiver_hbm, sems.at[1]),
    ]
    for copy in copies:
        copy.start()

    def planes(f, k):
        left, right = [], []
        near1 = [coarse_tile(m1, (f, p), k) for p in range(4)]
        near2 = [coarse_tile(m2, (f, p), k) for p in range(4)]
        far1, far2 = [], []
        for p in range(4):
            at = p * KT + k
            rows = slice(8 * (at % 2), 8 * (at % 2) + 8)
            far1.append(m1[f, 4, at // 2, rows, :])
            far2.append(m2[f, 4, at // 2, rows, :])
        for p in range(4):
            left.append(jnp.where(has_left, pick(gx_even, far2[p], far1[p]), 0.0))
        for p in range(4):
            left.append(jnp.where(has_left, pick(gx_even, near2[p], near1[p]), 0.0))
        for p in range(4):
            right.append(jnp.where(has_right, pick(gx_even, near1[p], near2[p]), 0.0))
        for p in range(4):
            right.append(jnp.where(has_right, pick(gx_even, far1[p], far2[p]), 0.0))
        return left + [coarse_ref[f, p, k] for p in range(VX)] + right

    for k in range(KT):
        source, receiver = planes(0, k), planes(1, k)
        for offset in range(NOFF):
            h = offset - REACH
            for a in range(VX // 2):
                image_ref[offset, a, k] = source[2 * a - h + REACH] * receiver[2 * a + h + REACH]
    for copy in copies:
        copy.wait()


def second_image_kernel(coarse_ref, m1, m2, before_ref, image_hbm, span, stage, sems):
    gx_even, has_left, has_right = flags_of()[:3]
    for f in range(2):
        for p in range(VX):
            span[f, p + REACH] = coarse_ref[f, p]
            for k in range(KT):
                a, b = m1[f, p, k], m2[f, p, k]
                span[f, p, k] = jnp.where(has_left, pick(gx_even, b, a), 0.0)
                span[f, p + REACH + VX, k] = jnp.where(has_right, pick(gx_even, a, b), 0.0)

    copies = []
    for a in range(VX // 2):
        for offset in range(NOFF):
            h = offset - REACH
            left, right = 2 * a - h + REACH, 2 * a + h + REACH
            for k in range(KT):
                value = before_ref[offset, a, k] + span[0, left, k] * span[1, right, k]
                stage[offset, a, :, k * 128 : (k + 1) * 128] = value
        copy = pltpu.make_async_copy(stage.at[:, a], image_hbm.at[:, a], sems.at[a])
        copy.start()
        copies.append(copy)
    for copy in copies:
        copy.wait()


VMEM = pl.BlockSpec(memory_space=pltpu.VMEM)
HBM = pl.BlockSpec(memory_space=pltpu.HBM)


def call(kernel, ins, outs, scratch=(), name=None, limit=12):
    return pl.pallas_call(
        kernel,
        out_shape=[jax.ShapeDtypeStruct(s, F32) for _, s in outs],
        in_specs=[s for s, _ in ins],
        out_specs=[s for s, _ in outs],
        scratch_shapes=list(scratch),
        name=name,
        cost_estimate=pl.CostEstimate(flops=0, bytes_accessed=0, transcendentals=0),
        compiler_params=pltpu.CompilerParams(vmem_limit_bytes=limit << 20),
    )(*[pltpu.with_memory_space_constraint(a, pltpu.HBM) if s is HBM else a for s, a in ins])


def vmem(*items):
    return [(VMEM, a) for a in items]


def hbm(*items):
    return [(HBM, a) for a in items]


def arrived(flops, *arrays):
    n = len(arrays)
    return pl.pallas_call(
        lambda *refs: None,
        out_shape=[jax.ShapeDtypeStruct(a.shape, F32) for a in arrays],
        in_specs=[VMEM] * n,
        out_specs=[VMEM] * n,
        input_output_aliases={i: i for i in range(n)},
        name="arrived",
        cost_estimate=pl.CostEstimate(flops=flops, bytes_accessed=0, transcendentals=0),
        compiler_params=pltpu.CompilerParams(vmem_limit_bytes=12 << 20),
    )(*arrays)


def dma(count):
    return pltpu.SemaphoreType.DMA((count,))


def inner(axis):
    return [(i, i ^ 1) for i in range(lax.axis_size(axis))]


def x_outer(near):
    nx, ny = lax.axis_size("gx"), lax.axis_size("gy")
    pairs = []
    for x in range(nx):
        for y in range(ny):
            other = x + 1 if x % 2 else x - 1
            if 0 <= other < nx:
                pairs.append((x * ny + y, other * ny + y))
            elif min(y, ny - 1 - y) < near:
                pairs.append((x * ny + y, x * ny + (y ^ 1)))
            else:
                pairs.append((x * ny + y, other % nx * ny + y))
    return pairs


def y_outer():
    nx, ny = lax.axis_size("gx"), lax.axis_size("gy")
    pairs = []
    for x in range(nx):
        for y in range(ny):
            other = y + 1 if y % 2 else y - 1
            if 0 <= other < ny:
                pairs.append((x * ny + y, x * ny + other))
            else:
                pairs.append((x * ny + y, (x ^ 1) * ny + y))
    return pairs


def along_x(m1, m2, near=4):
    return lax.ppermute(m1, "gx", inner("gx")), lax.ppermute(m2, ("gx", "gy"), x_outer(near))


def inner_y(m3):
    return lax.ppermute(m3, "gy", inner("gy"))


def outer_y(m4):
    return lax.ppermute(m4, ("gx", "gy"), y_outer())


def local(
    source_now,
    source_prev,
    receiver_now,
    receiver_prev,
    velocity_sq,
    source_cells,
    source_wavelet,
    receiver_cells,
    receiver_traces,
):
    block = (VX, VY, VZ)
    ext = pltpu.VMEM((VX, LT + 2, 32, 128), F32)
    whole = pltpu.VMEM(block, F32)
    m1, m2, m3, m4, source, receiver = call(
        first_pack_kernel,
        hbm(source_now, receiver_now),
        vmem(XSLAB, XSLAB, YSLAB, YSLAB, block, block),
        (dma(2),),
        name="pack",
    )
    g1, g2 = along_x(m1, m2)
    g3 = inner_y(m3)
    source_scratch = (
        ext,
        pltpu.SMEM(source_cells.shape, jnp.int32),
        pltpu.SMEM(source_wavelet.shape, F32),
        dma(2),
    )
    source_part, velocity = call(
        first_source_kernel,
        vmem(source) + hbm(source_prev, velocity_sq, source_cells, source_wavelet),
        vmem(FIELD, block),
        (
            ext,
            whole,
            pltpu.SMEM(source_cells.shape, jnp.int32),
            pltpu.SMEM(source_wavelet.shape, F32),
            dma(4),
        ),
        name="source1",
    )
    m4, source_part = lax.optimization_barrier((m4, source_part))
    g4 = outer_y(m4)
    receiver_part, inject = call(
        first_receiver_kernel,
        vmem(receiver, velocity)
        + hbm(receiver_prev, receiver_cells.reshape(32, 128), receiver_cells, receiver_traces),
        vmem(FIELD, FIELD),
        (
            ext,
            whole,
            pltpu.VMEM((32, 128), jnp.int32),
            pltpu.SMEM(receiver_cells.shape, jnp.int32),
            pltpu.SMEM(receiver_traces.shape, F32),
            pltpu.VMEM((1, 128), jnp.int32),
            pltpu.SMEM((1, 128), jnp.int32),
            dma(4),
            pltpu.SemaphoreType.DMA,
        ),
        name="receiver1",
    )
    source1, receiver1, m1, m2, m3, m4, coarse = call(
        first_halo_kernel,
        vmem(source_part, receiver_part, velocity, g2, g1, g3, g4),
        vmem(FIELD, FIELD, XSLAB_COARSE, XSLAB_COARSE, YSLAB, YSLAB, COARSE),
        name="halo1",
    )
    g4 = outer_y(m4)
    g1, g2 = along_x(m1, m2, near=2)
    g3 = inner_y(m3)
    source_part, receiver_part = call(
        second_local_kernel,
        vmem(source1, receiver1, source, receiver, velocity, inject) + hbm(source_cells, source_wavelet),
        vmem(FIELD, FIELD),
        source_scratch,
        name="local2",
    )
    g2, g4 = arrived(4300000000, g2, g4)
    source, receiver, last = call(
        second_halo_kernel,
        vmem(source_part, receiver_part, velocity, g2, g1, g3, g4),
        vmem(block, block, COARSE),
        (pltpu.VMEM(FIELD, F32),),
        name="halo2",
    )
    far = along_x(last, last)
    image, source_next, receiver_next = call(
        first_image_kernel,
        vmem(coarse, g1, g2, source, receiver),
        vmem((NOFF, VX // 2, KT, 8, 128)) + hbm(block, block),
        (dma(2),),
        name="image1",
    )
    (image,) = call(
        second_image_kernel,
        vmem(last, *far, image),
        hbm((NOFF, VX // 2, 8, KT * 128)),
        (
            pltpu.VMEM((2, 2 * REACH + VX, KT, 8, 128), F32),
            pltpu.VMEM((NOFF, VX // 2, 8, KT * 128), F32),
            dma(VX // 2),
        ),
        name="image2",
    )
    return source_next, receiver_next, image


def solution(mesh):
    field = P("gx", "gy", None)
    return jax.shard_map(
        local,
        mesh=mesh,
        in_specs=(field,) * 5 + (P(),) * 4,
        out_specs=(field, field, P(None, "gx", "gy", None)),
        check_vma=False,
    )
```

```python
import functools

import jax
import jax.numpy as jnp
from jax import lax
from jax.experimental import pallas as pl
from jax.experimental.pallas import tpu as pltpu
from jax.sharding import PartitionSpec as P

COEF = (-205.0 / 72.0, 8.0 / 5.0, -1.0 / 5.0, 8.0 / 315.0, -1.0 / 560.0)
NOFF = 17
REACH = 8
VX, VY, VZ = 8, 16, 1024
LT = VZ // 128
KT = LT // 2
F32 = jnp.float32

FIELD = (VX, LT, VY, 128)
XSLAB = (2, 4, LT, VY, 128)
XSLAB_COARSE = (2, 5, LT, VY, 128)
YSLAB = (2, 4, LT, 8, 128)
COARSE = (2, VX, KT, 8, 128)


def lane_iota(shape):
    return lax.broadcasted_iota(jnp.int32, shape, len(shape) - 1)


def pick(flag, yes, no):
    return jnp.where(flag, yes, no)


def compact_even(first, second):
    lane = lane_iota((8, 128))
    index = (2 * lane) & 127
    left = jnp.take_along_axis(first, index, axis=1)
    right = jnp.take_along_axis(second, index, axis=1)
    return jnp.where(lane < 64, left, right)


def coarse_tile(ref, lead, k):
    first = ref[lead + (2 * k, pl.ds(0, 8, stride=2), slice(None))]
    second = ref[lead + (2 * k + 1, pl.ds(0, 8, stride=2), slice(None))]
    return compact_even(first, second)


def pack_rows(top_ref, bottom_ref, f, l, low, high, gy_even):
    for p in range(VX):
        i, r = p % 4, 4 * (p // 4)
        top_ref[f, i, l, r : r + 4, :] = pick(gy_even, high[p], low[p])
        bottom_ref[f, i, l, r : r + 4, :] = pick(gy_even, low[p], high[p])


def first_pack_kernel(
    source_hbm,
    receiver_hbm,
    m1,
    m2,
    m3,
    m4,
    source_ref,
    receiver_ref,
    sems,
):
    gx_even = lax.rem(lax.axis_index("gx"), 2) == 0
    gy_even = lax.rem(lax.axis_index("gy"), 2) == 0
    copies = start_all(((source_hbm, source_ref), (receiver_hbm, receiver_ref)), sems)
    for f, ref in enumerate((source_ref, receiver_ref)):
        copies[f].wait()

        def tile(l, carry, f=f, ref=ref):
            lanes = pl.ds(pl.multiple_of(l * 128, 128), 128)
            for p in range(4):
                low = ref[p, :, lanes]
                high = ref[p + 4, :, lanes]
                m1[f, p, l] = pick(gx_even, high, low)
                m2[f, p, l] = pick(gx_even, low, high)
            low = [ref[p, 0:4, lanes] for p in range(VX)]
            high = [ref[p, 12:16, lanes] for p in range(VX)]
            pack_rows(m3, m4, f, l, low, high, gy_even)
            return carry

        lax.fori_loop(0, LT, tile, 0)


def star(ext, l, lane):
    centers = [ext[p, l + 1, 8 : 8 + VY, :] for p in range(VX)]
    out = []
    for p in range(VX):
        center = centers[p]
        after = ext[p, l + 2, 8 : 8 + VY, :]
        before = ext[p, l, 8 : 8 + VY, :]
        total = (3.0 * COEF[0]) * center
        for d in range(1, 5):
            near = pltpu.roll(jnp.where(lane >= d, center, after), 128 - d, 1)
            near = near + pltpu.roll(jnp.where(lane < 128 - d, center, before), d, 1)
            near = near + ext[p, l + 1, 8 + d : 8 + d + VY, :]
            near = near + ext[p, l + 1, 8 - d : 8 - d + VY, :]
            if p + d < VX:
                near = near + centers[p + d]
            if p - d >= 0:
                near = near + centers[p - d]
            total = total + COEF[d] * near
        out.append(total)
    return centers, out


def clear_ext(ext):
    def tile(p, carry):
        ext[p, :, 0:8, :] = jnp.zeros((LT + 2, 8, 128), F32)
        ext[p, :, 24:32, :] = jnp.zeros((LT + 2, 8, 128), F32)
        for l in (0, LT + 1):
            ext[p, l, 8:24, :] = jnp.zeros((VY, 128), F32)
        return carry

    lax.fori_loop(0, VX, tile, 0)


def lanes_of(l):
    return pl.ds(pl.multiple_of(l * 128, 128), 128)


def locate(cell):
    x = lax.shift_right_logical(cell, 17) - lax.axis_index("gx") * VX
    y = (lax.shift_right_logical(cell, 10) & 127) - lax.axis_index("gy") * VY
    return x, y, cell & 1023


def add_point(ref, cell, amount, velocity_ref=None):
    x, y, z = locate(cell)
    l = lax.shift_right_logical(z, 7)
    value = jnp.full((VY, 128), amount, F32)
    if velocity_ref is not None:
        value = value * velocity_ref[x, :, lanes_of(l)]
    row = lax.broadcasted_iota(jnp.int32, (VY, 128), 0)
    here = (row == y) & (lane_iota((VY, 128)) == (z & 127))
    ref[x, l] = ref[x, l] + jnp.where(here, value, 0.0)


def add_sources(ref, cells, wavelet, instant, velocity_ref):
    for j in range(cells.shape[0]):
        cell = cells[j]
        x, y, _ = locate(cell)
        here = (x >= 0) & (x < VX) & (y >= 0) & (y < VY)

        @pl.when(here)
        def _(cell=cell, j=j):
            add_point(ref, cell, wavelet[instant, j], velocity_ref)


def stencil(ext, older, velocity_ref, partial_ref, inject_ref=None):
    lane = lane_iota((VY, 128))

    def tile(l, carry):
        centers, totals = star(ext, l, lane)
        for p in range(VX):
            total = totals[p]
            if inject_ref is not None:
                total = total + inject_ref[p, l]
            v = velocity_ref[p, :, lanes_of(l)]
            partial_ref[p, l] = (2.0 * centers[p] - older[p, :, lanes_of(l)]) + v * total
        return carry

    lax.fori_loop(0, LT, tile, 0)


def start_all(pairs, sems):
    copies = [pltpu.make_async_copy(a, b, sems.at[i]) for i, (a, b) in enumerate(pairs)]
    for copy in copies:
        copy.start()
    return copies


def fill_ext(ext, ref):
    def tile(l, carry):
        for p in range(VX):
            ext[p, l + 1, 8 : 8 + VY, :] = ref[p, :, lanes_of(l)]
        return carry

    lax.fori_loop(0, LT, tile, 0)


def fill_ext_tiled(ext, ref):
    def tile(l, carry):
        for p in range(VX):
            ext[p, l + 1, 8 : 8 + VY, :] = ref[p, l]
        return carry

    lax.fori_loop(0, LT, tile, 0)


def first_receiver_kernel(
    now_ref,
    velocity_ref,
    prev_hbm,
    grid_hbm,
    cells_hbm,
    traces_hbm,
    partial_ref,
    inject_ref,
    ext,
    prev_ref,
    grid_ref,
    cells,
    traces,
    words_v,
    words_s,
    sems,
    word_sem,
):
    copies = start_all(
        ((grid_hbm, grid_ref), (cells_hbm, cells), (traces_hbm, traces), (prev_hbm, prev_ref)), sems
    )
    clear_ext(ext)
    fill_ext(ext, now_ref)

    copies[0].wait()
    x, y, _ = locate(grid_ref[...])
    inside = (x >= 0) & (x < VX) & (y >= 0) & (y < VY)
    bit = jnp.left_shift(1, lax.broadcasted_iota(jnp.int32, (32, 128), 0))
    words_v[...] = jnp.sum(jnp.where(inside, bit, 0), axis=0, keepdims=True)
    word_copy = pltpu.make_async_copy(words_v, words_s, word_sem)
    word_copy.start()

    def clear(l, carry):
        for p in range(VX):
            inject_ref[p, l] = jnp.zeros((VY, 128), F32)
        return carry

    lax.fori_loop(0, LT, clear, 0)
    copies[3].wait()
    stencil(ext, prev_ref, velocity_ref, partial_ref)
    for copy in copies[1:3]:
        copy.wait()
    word_copy.wait()

    def words_from(first, carry):
        words = [words_s[0, 8 * first + k] for k in range(8)]
        some = functools.reduce(lax.bitwise_or, words)

        @pl.when(some != 0)
        def _():
            for k in range(8):

                def one(bits, k=k):
                    low = bits & (-bits)
                    j = (31 - lax.clz(low)) * 128 + 8 * first + k
                    cell = cells[j]
                    add_point(partial_ref, cell, traces[0, j], velocity_ref)
                    add_point(inject_ref, cell, traces[1, j])
                    return bits & (bits - 1)

                lax.while_loop(lambda bits: bits != 0, one, words[k])

        return carry

    lax.fori_loop(0, 16, words_from, 0)


def first_source_kernel(
    now_ref,
    prev_hbm,
    velocity_hbm,
    cells_hbm,
    wavelet_hbm,
    partial_ref,
    velocity_ref,
    ext,
    prev_ref,
    cells,
    wavelet,
    sems,
):
    copies = start_all(
        ((velocity_hbm, velocity_ref), (prev_hbm, prev_ref), (cells_hbm, cells), (wavelet_hbm, wavelet)), sems
    )
    clear_ext(ext)
    fill_ext(ext, now_ref)
    for copy in copies:
        copy.wait()
    stencil(ext, prev_ref, velocity_ref, partial_ref)
    add_sources(partial_ref, cells, wavelet, 0, velocity_ref)


def source_kernel(
    fill, instant, now_ref, older_ref, velocity_ref, cells_hbm, wavelet_hbm, partial_ref, ext, cells, wavelet, sems
):
    copies = start_all(((cells_hbm, cells), (wavelet_hbm, wavelet)), sems)
    clear_ext(ext)
    fill(ext, now_ref)
    stencil(ext, older_ref, velocity_ref, partial_ref)
    for copy in copies:
        copy.wait()
    add_sources(partial_ref, cells, wavelet, instant, velocity_ref)


def second_local_kernel(
    source_ref,
    receiver_ref,
    source_old,
    receiver_old,
    velocity_ref,
    inject_ref,
    cells_hbm,
    wavelet_hbm,
    source_part,
    receiver_part,
    ext,
    cells,
    wavelet,
    sems,
):
    source_kernel(
        fill_ext_tiled, 1, source_ref, source_old, velocity_ref, cells_hbm, wavelet_hbm, source_part, ext, cells, wavelet, sems
    )
    fill_ext_tiled(ext, receiver_ref)
    stencil(ext, receiver_old, velocity_ref, receiver_part, inject_ref)


def row_factors():
    row = lax.broadcasted_iota(jnp.int32, (8, 128), 0)
    step = row & 3
    below = {d: jnp.where(step < d, COEF[d], 0.0) for d in range(1, 4)}
    above = {d: jnp.where(step >= 4 - d, COEF[d], 0.0) for d in range(1, 4)}
    return row < 4, below, above


def halo_terms(m1, m2, m3, m4, f, l, flags):
    gx_even, has_left, has_right, gy_even, has_below, has_above, (first, below_of, above_of) = flags
    left, right = [], []
    for p in range(4):
        a, b = m1[f, p, l], m2[f, p, l]
        left.append(jnp.where(has_left, pick(gx_even, b, a), 0.0))
        right.append(jnp.where(has_right, pick(gx_even, a, b), 0.0))
    lows, highs = [None] * VX, [None] * VX
    for i in range(4):
        a, b = m3[f, i, l], m4[f, i, l]
        low = jnp.where(has_below, pick(gy_even, b, a), 0.0)
        high = jnp.where(has_above, pick(gy_even, a, b), 0.0)
        below, above = COEF[4] * low, COEF[4] * high
        for d in range(1, 4):
            below = below + below_of[d] * pltpu.roll(low, 4 + d, 0)
            above = above + above_of[d] * pltpu.roll(high, 4 - d, 0)
        lows[i] = jnp.where(first, below, 0.0)
        lows[i + 4] = jnp.where(first, pltpu.roll(below, 4, 0), 0.0)
        highs[i] = jnp.where(first, 0.0, pltpu.roll(above, 4, 0))
        highs[i + 4] = jnp.where(first, 0.0, above)
    out = []
    for p in range(VX):
        total = jnp.concatenate((lows[p], highs[p]), axis=0)
        for d in range(1, 5):
            if p - d < 0:
                total = total + COEF[d] * left[4 + p - d]
            if p + d >= VX:
                total = total + COEF[d] * right[p + d - VX]
        out.append(total)
    return out


def flags_of():
    gx, gy = lax.axis_index("gx"), lax.axis_index("gy")
    return (
        lax.rem(gx, 2) == 0,
        gx > 0,
        gx < lax.axis_size("gx") - 1,
        lax.rem(gy, 2) == 0,
        gy > 0,
        gy < lax.axis_size("gy") - 1,
    )


def first_halo_kernel(
    source_part,
    receiver_part,
    velocity_ref,
    m2,
    m1,
    m3,
    m4,
    source_ref,
    receiver_ref,
    s1,
    s2,
    s3,
    s4,
    coarse_ref,
):
    flags = flags_of() + (row_factors(),)
    gx_even, gy_even = flags[0], flags[3]
    for f, (part, out) in enumerate(((source_part, source_ref), (receiver_part, receiver_ref))):

        def tile(l, carry, f=f, part=part, out=out):
            terms = halo_terms(m1, m2, m3, m4, f, l, flags)
            new = []
            for p in range(VX):
                value = part[p, l] + velocity_ref[p, :, lanes_of(l)] * terms[p]
                out[p, l] = value
                new.append(value)
            for p in range(4):
                s1[f, p, l] = pick(gx_even, new[p + 4], new[p])
                s2[f, p, l] = pick(gx_even, new[p], new[p + 4])
            pack_rows(s3, s4, f, l, [v[0:4] for v in new], [v[12:16] for v in new], gy_even)
            return carry

        lax.fori_loop(0, LT, tile, 0)
        for k in range(KT):
            low = [coarse_tile(out, (p,), k) for p in range(4)]
            high = [coarse_tile(out, (p + 4,), k) for p in range(4)]
            for p in range(4):
                coarse_ref[f, p, k] = low[p]
                coarse_ref[f, p + 4, k] = high[p]
                at = p * KT + k
                rows = slice(8 * (at % 2), 8 * (at % 2) + 8)
                s1[f, 4, at // 2, rows, :] = pick(gx_even, low[p], high[p])
                s2[f, 4, at // 2, rows, :] = pick(gx_even, high[p], low[p])


def second_halo_kernel(
    source_part,
    receiver_part,
    velocity_ref,
    m2,
    m1,
    m3,
    m4,
    source_ref,
    receiver_ref,
    coarse_ref,
    stage,
):
    flags = flags_of() + (row_factors(),)
    for f, (part, out) in enumerate(((source_part, source_ref), (receiver_part, receiver_ref))):

        def tile(l, carry, f=f, part=part, out=out):
            terms = halo_terms(m1, m2, m3, m4, f, l, flags)
            for p in range(VX):
                value = part[p, l] + velocity_ref[p, :, lanes_of(l)] * terms[p]
                out[p, :, lanes_of(l)] = value
                stage[p, l] = value
            return carry

        lax.fori_loop(0, LT, tile, 0)
        for k in range(KT):
            for p in range(VX):
                coarse_ref[f, p, k] = coarse_tile(stage, (p,), k)


def first_image_kernel(coarse_ref, m1, m2, source_ref, receiver_ref, image_ref, source_hbm, receiver_hbm, sems):
    gx_even, has_left, has_right = flags_of()[:3]
    copies = [
        pltpu.make_async_copy(source_ref, source_hbm, sems.at[0]),
        pltpu.make_async_copy(receiver_ref, receiver_hbm, sems.at[1]),
    ]
    for copy in copies:
        copy.start()

    def planes(f, k):
        left, right = [], []
        near1 = [coarse_tile(m1, (f, p), k) for p in range(4)]
        near2 = [coarse_tile(m2, (f, p), k) for p in range(4)]
        far1, far2 = [], []
        for p in range(4):
            at = p * KT + k
            rows = slice(8 * (at % 2), 8 * (at % 2) + 8)
            far1.append(m1[f, 4, at // 2, rows, :])
            far2.append(m2[f, 4, at // 2, rows, :])
        for p in range(4):
            left.append(jnp.where(has_left, pick(gx_even, far2[p], far1[p]), 0.0))
        for p in range(4):
            left.append(jnp.where(has_left, pick(gx_even, near2[p], near1[p]), 0.0))
        for p in range(4):
            right.append(jnp.where(has_right, pick(gx_even, near1[p], near2[p]), 0.0))
        for p in range(4):
            right.append(jnp.where(has_right, pick(gx_even, far1[p], far2[p]), 0.0))
        return left + [coarse_ref[f, p, k] for p in range(VX)] + right

    for k in range(KT):
        source, receiver = planes(0, k), planes(1, k)
        for offset in range(NOFF):
            h = offset - REACH
            for a in range(VX // 2):
                image_ref[offset, a, k] = source[2 * a - h + REACH] * receiver[2 * a + h + REACH]
    for copy in copies:
        copy.wait()


def second_image_kernel(coarse_ref, m1, m2, before_ref, image_hbm, span, stage, sems):
    gx_even, has_left, has_right = flags_of()[:3]
    for f in range(2):
        for p in range(VX):
            span[f, p + REACH] = coarse_ref[f, p]
            for k in range(KT):
                a, b = m1[f, p, k], m2[f, p, k]
                span[f, p, k] = jnp.where(has_left, pick(gx_even, b, a), 0.0)
                span[f, p + REACH + VX, k] = jnp.where(has_right, pick(gx_even, a, b), 0.0)

    copies = []
    for a in range(VX // 2):
        for offset in range(NOFF):
            h = offset - REACH
            left, right = 2 * a - h + REACH, 2 * a + h + REACH
            for k in range(KT):
                value = before_ref[offset, a, k] + span[0, left, k] * span[1, right, k]
                stage[offset, a, :, k * 128 : (k + 1) * 128] = value
        copy = pltpu.make_async_copy(stage.at[:, a], image_hbm.at[:, a], sems.at[a])
        copy.start()
        copies.append(copy)
    for copy in copies:
        copy.wait()


VMEM = pl.BlockSpec(memory_space=pltpu.VMEM)
HBM = pl.BlockSpec(memory_space=pltpu.HBM)


def call(kernel, ins, outs, scratch=(), name=None, limit=12):
    return pl.pallas_call(
        kernel,
        out_shape=[jax.ShapeDtypeStruct(s, F32) for _, s in outs],
        in_specs=[s for s, _ in ins],
        out_specs=[s for s, _ in outs],
        scratch_shapes=list(scratch),
        name=name,
        cost_estimate=pl.CostEstimate(flops=0, bytes_accessed=0, transcendentals=0),
        compiler_params=pltpu.CompilerParams(vmem_limit_bytes=limit << 20),
    )(*[pltpu.with_memory_space_constraint(a, pltpu.HBM) if s is HBM else a for s, a in ins])


def vmem(*items):
    return [(VMEM, a) for a in items]


def hbm(*items):
    return [(HBM, a) for a in items]


def arrived(flops, *arrays):
    n = len(arrays)
    return pl.pallas_call(
        lambda *refs: None,
        out_shape=[jax.ShapeDtypeStruct(a.shape, F32) for a in arrays],
        in_specs=[VMEM] * n,
        out_specs=[VMEM] * n,
        input_output_aliases={i: i for i in range(n)},
        name="arrived",
        cost_estimate=pl.CostEstimate(flops=flops, bytes_accessed=0, transcendentals=0),
        compiler_params=pltpu.CompilerParams(vmem_limit_bytes=12 << 20),
    )(*arrays)


def dma(count):
    return pltpu.SemaphoreType.DMA((count,))


def inner(axis):
    return [(i, i ^ 1) for i in range(lax.axis_size(axis))]


def x_outer(near):
    nx, ny = lax.axis_size("gx"), lax.axis_size("gy")
    pairs = []
    for x in range(nx):
        for y in range(ny):
            other = x + 1 if x % 2 else x - 1
            if 0 <= other < nx:
                pairs.append((x * ny + y, other * ny + y))
            elif min(y, ny - 1 - y) < near:
                pairs.append((x * ny + y, x * ny + (y ^ 1)))
            else:
                pairs.append((x * ny + y, other % nx * ny + y))
    return pairs


def y_outer():
    nx, ny = lax.axis_size("gx"), lax.axis_size("gy")
    pairs = []
    for x in range(nx):
        for y in range(ny):
            other = y + 1 if y % 2 else y - 1
            if 0 <= other < ny:
                pairs.append((x * ny + y, x * ny + other))
            else:
                pairs.append((x * ny + y, (x ^ 1) * ny + y))
    return pairs


def along_x(m1, m2, near=4):
    return lax.ppermute(m1, "gx", inner("gx")), lax.ppermute(m2, ("gx", "gy"), x_outer(near))


def inner_y(m3):
    return lax.ppermute(m3, "gy", inner("gy"))


def outer_y(m4):
    return lax.ppermute(m4, ("gx", "gy"), y_outer())


def local(
    source_now,
    source_prev,
    receiver_now,
    receiver_prev,
    velocity_sq,
    source_cells,
    source_wavelet,
    receiver_cells,
    receiver_traces,
):
    block = (VX, VY, VZ)
    ext = pltpu.VMEM((VX, LT + 2, 32, 128), F32)
    whole = pltpu.VMEM(block, F32)
    m1, m2, m3, m4, source, receiver = call(
        first_pack_kernel,
        hbm(source_now, receiver_now),
        vmem(XSLAB, XSLAB, YSLAB, YSLAB, block, block),
        (dma(2),),
        name="pack",
    )
    g1, g2 = along_x(m1, m2)
    g3 = inner_y(m3)
    source_scratch = (
        ext,
        pltpu.SMEM(source_cells.shape, jnp.int32),
        pltpu.SMEM(source_wavelet.shape, F32),
        dma(2),
    )
    source_part, velocity = call(
        first_source_kernel,
        vmem(source) + hbm(source_prev, velocity_sq, source_cells, source_wavelet),
        vmem(FIELD, block),
        (
            ext,
            whole,
            pltpu.SMEM(source_cells.shape, jnp.int32),
            pltpu.SMEM(source_wavelet.shape, F32),
            dma(4),
        ),
        name="source1",
    )
    m4, source_part = lax.optimization_barrier((m4, source_part))
    g4 = outer_y(m4)
    receiver_part, inject = call(
        first_receiver_kernel,
        vmem(receiver, velocity)
        + hbm(receiver_prev, receiver_cells.reshape(32, 128), receiver_cells, receiver_traces),
        vmem(FIELD, FIELD),
        (
            ext,
            whole,
            pltpu.VMEM((32, 128), jnp.int32),
            pltpu.SMEM(receiver_cells.shape, jnp.int32),
            pltpu.SMEM(receiver_traces.shape, F32),
            pltpu.VMEM((1, 128), jnp.int32),
            pltpu.SMEM((1, 128), jnp.int32),
            dma(4),
            pltpu.SemaphoreType.DMA,
        ),
        name="receiver1",
    )
    source1, receiver1, m1, m2, m3, m4, coarse = call(
        first_halo_kernel,
        vmem(source_part, receiver_part, velocity, g2, g1, g3, g4),
        vmem(FIELD, FIELD, XSLAB_COARSE, XSLAB_COARSE, YSLAB, YSLAB, COARSE),
        name="halo1",
    )
    g4 = outer_y(m4)
    g1, g2 = along_x(m1, m2, near=2)
    g3 = inner_y(m3)
    source_part, receiver_part = call(
        second_local_kernel,
        vmem(source1, receiver1, source, receiver, velocity, inject) + hbm(source_cells, source_wavelet),
        vmem(FIELD, FIELD),
        source_scratch,
        name="local2",
    )
    g2, g4 = arrived(4300000000, g2, g4)
    source, receiver, last = call(
        second_halo_kernel,
        vmem(source_part, receiver_part, velocity, g2, g1, g3, g4),
        vmem(block, block, COARSE),
        (pltpu.VMEM(FIELD, F32),),
        name="halo2",
    )
    far = along_x(last, last)
    image, source_next, receiver_next = call(
        first_image_kernel,
        vmem(coarse, g1, g2, source, receiver),
        vmem((NOFF, VX // 2, KT, 8, 128)) + hbm(block, block),
        (dma(2),),
        name="image1",
    )
    (image,) = call(
        second_image_kernel,
        vmem(last, *far, image),
        hbm((NOFF, VX // 2, 8, KT * 128)),
        (
            pltpu.VMEM((2, 2 * REACH + VX, KT, 8, 128), F32),
            pltpu.VMEM((NOFF, VX // 2, 8, KT * 128), F32),
            dma(VX // 2),
        ),
        name="image2",
    )
    return source_next, receiver_next, image


def solution(mesh):
    field = P("gx", "gy", None)
    return jax.shard_map(
        local,
        mesh=mesh,
        in_specs=(field,) * 5 + (P(),) * 4,
        out_specs=(field, field, P(None, "gx", "gy", None)),
        check_vma=False,
    )
```
